256 devices in a mesh: wa: 128 (over z, x_hi, y, core), gy: 2 (over x_lo).
Axes of the slice: x: 4 (x_hi: 2, x_lo: 2; x = x_hi * 2 + x_lo), y: 4, z: 8, core: 2. Of those that a mesh axis runs over, the one named last changes fastest.
Arguments:
- input_moments: float32 [120, 1024, 256], P(None, 'wa', 'gy'), may hold values from -6 to 6
- solid_cell_mask: int32 [1024, 256], P('wa', 'gy'), may hold values 0 or 1
- collision_coefficients: float32 [120, 120], replicated, may hold values from -0.5 to 0.5
- relaxation_rates: float32 [120], replicated, may hold values from 0.1 to 1
Outputs:
- final_state: float32 [120, 1024, 256], P(None, 'wa', 'gy')
The draws below stay inside these ranges and needn't reach their ends.
All inputs are finite; a program needn't handle non-finite values. No bound on the sum of `solid_cell_mask` on one device may be relied on, other than what follows from the above.
Results may differ from the reference program's by a relative error of at most 0.0003.
Values sent between devices are 32-bit elements; how exact they have to be, the bound alone decides.
A program may use at most 64 MiB of HBM per device.

```python
import math
import jax
import jax.numpy as jnp
import numpy as np
from jax import lax

DEG = 7
MOMENT_COUNT = 120
ITERS = 2
NX = 1024
NY = 256


def touch_ends(drawn, rng, low, top_value):
    spot = [jax.random.randint(jax.random.fold_in(rng, axis), (), 0, length) for axis, length in enumerate(drawn.shape)]
    main_axis = drawn.shape.index(max(drawn.shape))
    next_to = spot[:main_axis] + [(spot[main_axis] + 1) % drawn.shape[main_axis]] + spot[main_axis + 1:]
    return drawn.at[tuple(spot)].set(low).at[tuple(next_to)].set(top_value)


def block_scale(rng, extent, cuts, smallest, largest):
    def one(axis_at, parts):
        draws = jax.random.uniform(jax.random.fold_in(jax.random.fold_in(rng, 6), axis_at), (parts,), jnp.float32, smallest / len(cuts), largest / len(cuts))
        return jnp.repeat(jnp.exp(draws), extent[axis_at] // parts).reshape((-1,) + (1,) * (len(extent) - axis_at - 1))

    gain = one(*cuts[0])
    for cut in cuts[1:]:
        gain = gain * one(*cut)
    return gain


def scatter_about(key, dims, scale, reach, shards=(), kind=jnp.bfloat16):
    values = scale * jax.random.normal(key, dims, jnp.float32)
    if shards:
        values = values * block_scale(key, dims, shards, -0.22, 0.18)
    return jnp.clip(values, -reach, reach).astype(kind)


def setup_inputs(seed: int = 0) -> dict:
    key_list = jax.random.split(jax.random.key(seed), 5)
    return {
        "input_moments": scatter_about(key_list[0], (MOMENT_COUNT, NX, NY), 1.0, 6.0, ((1, 128), (2, 2)), jnp.float32),
        "solid_cell_mask": touch_ends((jax.random.randint(key_list[1], (NX, NY), 0, 8) < 1).astype(jnp.int32), jax.random.fold_in(key_list[1], 1), 0, 1),
        "collision_coefficients": scatter_about(key_list[2], (MOMENT_COUNT, MOMENT_COUNT), MOMENT_COUNT ** -0.5, 0.5, (), jnp.float32),
        "relaxation_rates": jnp.clip(jnp.exp(jax.random.uniform(key_list[3], (MOMENT_COUNT,), jnp.float32, math.log(0.1), math.log(1.0))), 0.1, 1.0),
    }


highest_degree = lax.Precision.HIGHEST
axial_step = 0.2
cross_step = 0.2
collide_step = 0.5

def moment_table():
    entries = []
    for degree_now in range(DEG + 1):
        for first_k in range(degree_now, -1, -1):
            for second_k in range(degree_now - first_k, -1, -1):
                entries.append((first_k, second_k, degree_now - first_k - second_k))
    return entries

def hermite_value(order, point):
    previous = 1.0
    current_moments = point
    for level in range(1, order):
        previous, current_moments = (current_moments, point * current_moments - level * previous)
    return current_moments

def largest_root(order):
    upper = 2.0 * math.sqrt(order) + 1.0
    value_high = hermite_value(order, upper)
    lower = upper
    for trial in range(100000):
        lower = lower - 0.001
        value_low = hermite_value(order, lower)
        if (value_low > 0.0) != (value_high > 0.0):
            break
        upper = lower
        value_high = value_low
    for repeat in range(80):
        middle = 0.5 * (lower + upper)
        value_mid = hermite_value(order, middle)
        if (value_mid > 0.0) == (value_high > 0.0):
            upper = middle
            value_high = value_mid
        else:
            lower = middle
    return 0.5 * (lower + upper)

def coupling(entries, lookup, direction):
    matrix = np.zeros((len(entries), len(entries)), dtype=np.float32)
    for position, moment in enumerate(entries):
        raised = list(moment)
        raised[direction] += 1
        raised = tuple(raised)
        if raised in lookup:
            partner = lookup[raised]
            matrix[position, partner] = math.sqrt(moment[direction] + 1)
            matrix[partner, position] = math.sqrt(moment[direction] + 1)
    return matrix

def to_float(table):
    return jnp.asarray(table, dtype=jnp.float32)

def operator_tables():
    entries = moment_table()
    number = len(entries)
    lookup = {moment: position for position, moment in enumerate(entries)}
    axial_matrix = coupling(entries, lookup, 0)
    cross_matrix = coupling(entries, lookup, 1)
    degrees = np.array([sum(moment) for moment in entries])
    degree_band_mask = ((np.abs(degrees[:, None] - degrees[None, :]) <= 1) & (degrees[:, None] >= 2) & (degrees[None, :] >= 2)).astype(np.float32)
    unit_rows = [lookup[1, 0, 0], lookup[0, 1, 0], lookup[0, 0, 1]]
    first_selection = np.zeros((number, number), dtype=np.float32)
    second_selection = np.zeros((number, number), dtype=np.float32)
    moment_weights = np.zeros(number, dtype=np.float32)
    for position, moment in enumerate(entries):
        if sum(moment) == 2:
            raised = [direction for direction in range(3) for repeat in range(moment[direction])]
            first_selection[position, unit_rows[raised[0]]] = 1.0
            second_selection[position, unit_rows[raised[1]]] = 1.0
            moment_weights[position] = 1.0 / math.sqrt(2.0) if raised[0] == raised[1] else 1.0
    relaxed = (degrees >= 2).astype(np.float32)
    density = (degrees == 0).astype(np.float32)
    speed_bound = largest_root(DEG + 1)
    return (to_float(axial_matrix), to_float(cross_matrix), to_float(degree_band_mask), to_float(first_selection), to_float(second_selection), to_float(moment_weights), to_float(relaxed), to_float(density), speed_bound)

def wave_numbers(length):
    position = jnp.arange(length, dtype=jnp.int32)
    signed = jnp.where(position < length // 2, position, position - length)
    return signed.astype(jnp.float32) * (axial_step * 2.0 * math.pi / length)

def phase_series(real_part, imag_part, axial_matrix, wave_scale):
    total_real, total_imag = (real_part, imag_part)
    term_real, term_imag = (real_part, imag_part)
    for term_order in range(1, 5):
        pushed_real = jnp.einsum('js,suv->juv', axial_matrix, term_real, precision=highest_degree) * wave_scale[None, :, None]
        pushed_imag = jnp.einsum('js,suv->juv', axial_matrix, term_imag, precision=highest_degree) * wave_scale[None, :, None]
        term_real, term_imag = (pushed_imag / term_order, -pushed_real / term_order)
        total_real = total_real + term_real
        total_imag = total_imag + term_imag
    return (total_real, total_imag)

def cross_update(current_moments, lower_rim, upper_rim, cross_matrix, speed_bound):
    central = jnp.einsum('js,suv->juv', cross_matrix, upper_rim - lower_rim, precision=highest_degree)
    return current_moments - cross_step * (0.5 * central - 0.5 * speed_bound * (upper_rim - 2.0 * current_moments + lower_rim))

def apply_walls(current_moments, mask_float, density):
    return current_moments * (1.0 - mask_float[None, :, :] * (1.0 - density)[:, None, None])

def apply_collisions(current_moments, collision_band, first_selection, second_selection, moment_weights, relaxation_applied):
    first_part = jnp.einsum('js,suv->juv', first_selection, current_moments, precision=highest_degree)
    second_part = jnp.einsum('js,suv->juv', second_selection, current_moments, precision=highest_degree)
    target = moment_weights[:, None, None] * first_part * second_part
    moment_mixing = jnp.einsum('js,suv->juv', collision_band, current_moments, precision=highest_degree)
    return current_moments + collide_step * (moment_mixing - relaxation_applied[:, None, None] * (current_moments - target))

def reference(input_moments, solid_cell_mask, collision_coefficients, relaxation_rates):
    axial_matrix, cross_matrix, degree_band_mask, first_selection, second_selection, moment_weights, relaxed, density, speed_bound = operator_tables()
    collision_band = collision_coefficients * degree_band_mask
    relaxation_applied = relaxation_rates * relaxed
    length = input_moments.shape[1]
    wave_scale = wave_numbers(length)
    mask_float = solid_cell_mask.astype(jnp.float32)
    current_moments = input_moments
    for step_index in range(ITERS):
        spectrum = jnp.fft.fft(current_moments, axis=1)
        real_part = jnp.real(spectrum).astype(jnp.float32)
        imag_part = jnp.imag(spectrum).astype(jnp.float32)
        total_real, total_imag = phase_series(real_part, imag_part, axial_matrix, wave_scale)
        current_moments = jnp.real(jnp.fft.ifft(lax.complex(total_real, total_imag), axis=1)).astype(jnp.float32)
        padded = jnp.pad(current_moments, ((0, 0), (0, 0), (1, 1)))
        current_moments = cross_update(current_moments, padded[:, :, :-2], padded[:, :, 2:], cross_matrix, speed_bound)
        current_moments = apply_walls(current_moments, mask_float, density)
        current_moments = apply_collisions(current_moments, collision_band, first_selection, second_selection, moment_weights, relaxation_applied)
    return current_moments
```

```python
import functools
import math

import jax
import jax.numpy as jnp
import ml_dtypes
import numpy as np
from jax import lax
from jax.experimental import pallas as pl
from jax.experimental.pallas import tpu as pltpu
from jax.sharding import PartitionSpec as P

DEG = 7
AXIAL_STEP = 0.2
CROSS_STEP = 0.2
COLLIDE_STEP = 0.5
NX = 1024
LINES = 128
OWN = 8
LANES = 128
MOMENTS = 120
MASK_LANE = 120
HALF = 72
BLOCKS = HALF // 8
ROOT_HALF = math.sqrt(0.5)

F32 = jnp.float32
BF16 = jnp.bfloat16
MESH = pl.DeviceIdType.MESH


def moment_table():
    entries = []
    for degree in range(DEG + 1):
        for k1 in range(degree, -1, -1):
            for k2 in range(degree - k1, -1, -1):
                entries.append((k1, k2, degree - k1 - k2))
    return entries


def hermite(order, point):
    previous, current = 0.0, 1.0
    for level in range(order):
        previous, current = current, point * current - level * previous
    return current


def hermite_roots(order):
    roots, step = [], 1.0 / 128
    low = -(2.0 * math.sqrt(order) + 1.0) - step / 3
    while len(roots) < order:
        high = low + step
        if (hermite(order, low) > 0) != (hermite(order, high) > 0):
            a, b = low, high
            for _ in range(80):
                middle = 0.5 * (a + b)
                if (hermite(order, middle) > 0) == (hermite(order, a) > 0):
                    a = middle
                else:
                    b = middle
            roots.append(0.5 * (a + b))
        low = high
    return roots


def coupling(entries, lookup, direction):
    matrix = np.zeros((LANES, LANES))
    for position, moment in enumerate(entries):
        raised = list(moment)
        raised[direction] += 1
        partner = lookup.get(tuple(raised))
        if partner is not None:
            matrix[position, partner] = matrix[partner, position] = math.sqrt(raised[direction])
    return matrix


def axial_modes(lookup):
    values = np.zeros(LANES)
    vectors = np.zeros((LANES, LANES))
    column = 0
    for k2 in range(DEG + 1):
        for k3 in range(DEG + 1 - k2):
            size = DEG + 1 - k2 - k3
            for root in hermite_roots(size):
                entry = [hermite(k, root) / math.sqrt(math.factorial(k)) for k in range(size)]
                norm = math.sqrt(sum(v * v for v in entry))
                for k in range(size):
                    vectors[lookup[k, k2, k3], column] = entry[k] / norm
                values[column] = root
                column += 1
    return values, vectors


def parts(table):
    high = table.astype(np.float32).astype(ml_dtypes.bfloat16)
    low = (table - high.astype(np.float64)).astype(np.float32).astype(ml_dtypes.bfloat16)
    return high, low


def right_factor(table):
    high, low = parts(table)
    return np.block([[high, low], [high, np.zeros_like(low)]])


@functools.cache
def tables():
    entries = moment_table()
    lookup = {moment: position for position, moment in enumerate(entries)}
    values, modes = axial_modes(lookup)
    a2 = coupling(entries, lookup, 1)
    speed = hermite_roots(DEG + 1)[-1]
    eye = np.eye(LANES)

    high, low = parts(modes.T)
    to_modes = np.concatenate([high, high, low], axis=1)

    k1 = np.arange(HALF)
    used = k1 <= 64
    weight = np.where(used, np.where((k1 == 0) | (k1 == 64), 1.0, 2.0), 0.0) / NX
    line = np.arange(LINES)
    forward, inverse = [], []
    for own in range(OWN):
        phase = (((OWN * line + own)[:, None] * k1[None, :]) % NX) * (2 * math.pi / NX)
        cosine, sine = np.cos(phase) * used, np.sin(phase) * used
        forward.append(np.concatenate(parts(np.concatenate([cosine.T, -sine.T], axis=0)), axis=1))
        inverse.append(np.concatenate(parts(np.concatenate([cosine * weight, -sine * weight], axis=1)), axis=0))
    forward, inverse = np.stack(forward), np.stack(inverse)

    wave = k1[None, :] + 128 * np.arange(8)[:, None]
    wave = np.where(wave < NX // 2, wave, wave - NX) * (AXIAL_STEP * 2 * math.pi / NX)
    angle = (wave[:, :, None] * values) * used[None, :, None]
    series = np.stack([1 - angle**2 / 2 + angle**4 / 24, -(angle - angle**3 / 6)])
    series = series.astype(np.float32)

    here = modes.T * (1 - CROSS_STEP * speed)
    upper = modes.T @ (0.5 * CROSS_STEP * (speed * eye - a2))
    lower = modes.T @ (0.5 * CROSS_STEP * (speed * eye + a2))
    cross = np.stack(
        [np.concatenate([right_factor(m) for m in order]) for order in ((here, upper, lower), (here, lower, upper))]
    )

    degrees = np.array([sum(moment) for moment in entries] + [0] * (LANES - MOMENTS))
    band = (np.abs(degrees[:, None] - degrees[None, :]) <= 1) & (degrees[:, None] >= 2) & (degrees[None, :] >= 2)
    first, second = np.zeros((LANES, LANES)), np.zeros((LANES, LANES))
    rows = np.zeros((8, LANES), np.float32)
    units = [lookup[1, 0, 0], lookup[0, 1, 0], lookup[0, 0, 1]]
    for position, moment in enumerate(entries):
        if sum(moment) == 2:
            d = [direction for direction in range(3) for _ in range(moment[direction])]
            first[units[d[0]], position] = 1.0
            second[units[d[1]], position] = 1.0
            rows[0, position] = COLLIDE_STEP * (ROOT_HALF if d[0] == d[1] else 1.0)
    pick = np.concatenate([first, second], axis=1)
    pick = np.concatenate([pick, pick], axis=0).astype(ml_dtypes.bfloat16)
    rows[1] = COLLIDE_STEP * (degrees >= 2)
    band = (band * COLLIDE_STEP).astype(np.float32)
    modes_right = right_factor(modes)
    return dict(
        to_modes=to_modes, forward=forward, inverse=inverse, series=series, cross=cross, band=band, rows=rows, pick=pick,
        modes_right=modes_right,
    )


def split(a):
    high = a.astype(BF16)
    return high, (a - high.astype(F32)).astype(BF16)


def fold(a):
    return a[:, :LANES] + a[:, LANES:]


def add(a, b):
    return (a[0] + b[0], a[1] + b[1])


def sub(a, b):
    return (a[0] - b[0], a[1] - b[1])


def quarter(a, sign):
    return (-a[1], a[0]) if sign > 0 else (a[1], -a[0])


def fourier4(v, sign):
    s, d = add(v[0], v[2]), sub(v[0], v[2])
    t, e = add(v[1], v[3]), quarter(sub(v[1], v[3]), sign)
    return [add(s, t), add(d, e), sub(s, t), sub(d, e)]


def fourier8(v, sign):
    even, odd = fourier4(v[0::2], sign), fourier4(v[1::2], sign)
    turned = [
        odd[0],
        ((odd[1][0] - sign * odd[1][1]) * ROOT_HALF, (odd[1][1] + sign * odd[1][0]) * ROOT_HALF),
        quarter(odd[2], sign),
        ((-odd[3][0] - sign * odd[3][1]) * ROOT_HALF, (-odd[3][1] + sign * odd[3][0]) * ROOT_HALF),
    ]
    return [add(a, b) for a, b in zip(even, turned)] + [sub(a, b) for a, b in zip(even, turned)]


def device_at(place):
    chip, core = place // 2, place % 2
    x_hi = chip // 32
    turn = chip % 32
    turn = turn + x_hi * (31 - 2 * turn)
    z = turn // 4
    y = turn % 4
    y = y + (z % 2) * (3 - 2 * y)
    return ((z * 2 + x_hi) * 4 + y) * 2 + core


def place_of(device):
    core, y, x_hi, z = device % 2, (device // 2) % 4, (device // 8) % 2, device // 16
    turn = z * 4 + y + (z % 2) * (3 - 2 * y)
    return (x_hi * 32 + turn + x_hi * (31 - 2 * turn)) * 2 + core


def kernel(
    x_ref, mask_ref, c_ref, rate_ref,
    to_modes_h, forward_h, inverse_h, series_h, cross_h, band_h, rows_h, pick_h, modes_h,
    out_ref,
    to_modes, forward, inverse, series, cross, band, rows, pick, modes,
    send1, recv1, send2, recv2, lines, beside, wall, spectrum, square, rate_row, collide,
    table_sem, send_sem, recv_sem, edge_send, edge_recv, near_send, near_recv,
):
    me, slab = lax.axis_index("wa"), lax.axis_index("gy")
    place = place_of(me)
    my_line = place + slab * (LINES - 1 - 2 * place)
    is_edge = place // (LINES - 1)
    next_wa, next_gy = device_at(place + 1 - is_edge), slab + is_edge * (1 - 2 * slab)
    is_first = 1 - (place + LINES - 1) // LINES
    prev_wa, prev_gy = device_at(place - 1 + is_first), slab + is_first * (1 - 2 * slab)

    barrier = pltpu.get_barrier_semaphore()

    @pl.loop(1, LINES)
    def _(step):
        pl.semaphore_signal(barrier, inc=1, device_id=((me + step) % LINES, slab), device_id_type=MESH)

    pl.semaphore_signal(barrier, inc=1, device_id=(me, 1 - slab), device_id_type=MESH)

    loads = [
        pltpu.make_async_copy(src, dst, table_sem.at[i])
        for i, (src, dst) in enumerate(
            [(to_modes_h, to_modes), (forward_h, forward), (series_h, series), (inverse_h, inverse), (cross_h.at[slab], cross.at[0]),
             (cross_h.at[0], cross.at[1]), (band_h, band), (rows_h, rows), (pick_h, pick), (modes_h, modes)]
        )
    ]
    for load in loads:
        load.start()
    loads[0].wait()

    row = lax.broadcasted_iota(jnp.int32, (LANES, LANES), 0)
    lane = lax.broadcasted_iota(jnp.int32, (LANES, LANES), 1)

    @pl.loop(0, OWN)
    def _(own):
        cells = x_ref[pl.ds(own, MOMENTS, stride=OWN), :]
        cells = jnp.concatenate([cells, jnp.zeros((LANES - MOMENTS, LANES), F32)], axis=0)
        high, low = split(cells)
        turned = jnp.dot(to_modes[...], jnp.concatenate([high, low, high], axis=0), preferred_element_type=F32)
        flags = mask_ref[pl.ds(own, 1), :].astype(F32)
        turned = jnp.where(row == MASK_LANE, flags, turned)
        send1[pl.ds(own, LINES, stride=OWN), :] = turned.T

    pl.semaphore_wait(barrier, LINES)

    @pl.loop(1, LINES)
    def _(step):
        target = (me + step) % LINES
        target_place = place_of(target)
        target_line = target_place + slab * (LINES - 1 - 2 * target_place)
        pltpu.make_async_remote_copy(
            src_ref=send1.at[pl.ds(pl.multiple_of(target_line * OWN, OWN), OWN), :],
            dst_ref=recv1.at[pl.ds(pl.multiple_of(me * OWN, OWN), OWN), :],
            send_sem=send_sem.at[0],
            recv_sem=recv_sem.at[0],
            device_id=(target, slab),
            device_id_type=MESH,
        ).start()

    recv1[pl.ds(pl.multiple_of(me * OWN, OWN), OWN), :] = send1[pl.ds(pl.multiple_of(my_line * OWN, OWN), OWN), :]

    for load in loads[1:]:
        load.wait()
    square[...] = jnp.zeros_like(square)
    square[:MOMENTS, :MOMENTS] = c_ref[...]
    rate_row[...] = jnp.zeros_like(rate_row)
    rate_row[:, :MOMENTS] = rate_ref[...]
    rates = rate_row[...] * rows[1:2, :]
    linear = (square[...] * band[...]).T + jnp.where(row == lane, 1.0 - rates, 0.0)
    high, low = split(linear)
    collide[...] = jnp.concatenate(
        [jnp.concatenate([high, low], axis=1), jnp.concatenate([high, jnp.zeros_like(low)], axis=1)], axis=0
    )
    drive = rate_row[...] * rows[0:1, :]

    def finish(here, after, before, factor, keep):
        operand = jnp.concatenate([*split(here), *split(after), *split(before)], axis=1)
        f = fold(jnp.dot(operand, factor, preferred_element_type=F32)) * keep
        operand = jnp.concatenate(split(f), axis=1)
        mixed = fold(jnp.dot(operand, collide[...], preferred_element_type=F32))
        chosen = jnp.dot(operand, pick[...], preferred_element_type=F32)
        return mixed + drive * (chosen[:, :LANES] * chosen[:, LANES:])

    def to_spectrum(own, cells):
        high, low = split(cells)
        table = forward[own]
        operand = jnp.concatenate([table[:, :LANES], table], axis=1)
        spectrum[own] = jnp.dot(operand, jnp.concatenate([high, low, high], axis=0), preferred_element_type=F32)

    def advance():
        @pl.loop(0, BLOCKS)
        def _(block):
            at = pl.multiple_of(block * 8, 8)
            re, im = pl.ds(at, 8), pl.ds(pl.multiple_of(HALF + at, 8), 8)
            f = fourier8([(spectrum[own, re, :], spectrum[own, im, :]) for own in range(OWN)], -1)
            h = []
            for k, (fr, fi) in enumerate(f):
                pr, pi = series[0, k, re, :], series[1, k, re, :]
                h.append((pr * fr - pi * fi, pr * fi + pi * fr))
            for own, (ur, ui) in enumerate(fourier8(h, 1)):
                spectrum[own, re, :] = ur
                spectrum[own, im, :] = ui

    def from_spectrum(own):
        high, low = split(spectrum[own])
        table = inverse[own]
        main = jnp.dot(table[:LINES], jnp.concatenate([high, low], axis=1), preferred_element_type=F32)
        return fold(main) + jnp.dot(table[LINES:], high, preferred_element_type=F32)

    rest = pl.ds(0, (LINES - 1) * OWN)
    pltpu.make_async_copy(recv1.at[rest, :], recv1.at[rest, :], recv_sem.at[0]).wait()

    @pl.loop(0, OWN)
    def _(own):
        cells = recv1[pl.ds(own, LINES, stride=OWN), :]
        flags = jnp.broadcast_to(cells[:, MASK_LANE : MASK_LANE + 1], (LINES, LANES))
        wall[own] = jnp.where(lane == 0, 1.0, 1.0 - flags)
        to_spectrum(own, cells)

    advance()

    def near(own, which):
        slot = 1 - is_first if which else is_edge
        return pltpu.make_async_remote_copy(
            src_ref=lines.at[own],
            dst_ref=beside.at[slot, own],
            send_sem=near_send.at[which, own],
            recv_sem=near_recv.at[slot, own],
            device_id=(prev_wa, prev_gy) if which else (next_wa, next_gy),
            device_id_type=MESH,
        )

    @pl.loop(0, OWN)
    def _(own):
        lines[own] = from_spectrum(own)
        near(own, 0).start()
        near(own, 1).start()

    inside = 1.0 - is_first.astype(F32)

    @pl.loop(0, OWN)
    def _(own):
        for slot in range(2):
            pltpu.make_async_copy(lines.at[own], beside.at[slot, own], near_recv.at[slot, own]).wait()
        f = finish(lines[own], beside[1, own], beside[0, own] * inside, cross[0], wall[own])
        f = fold(jnp.dot(jnp.concatenate(split(f), axis=1), modes[...], preferred_element_type=F32))
        to_spectrum(own, f)

    advance()

    @pl.loop(0, OWN)
    def _(own):
        send2[pl.ds(own, LINES, stride=OWN), :] = from_spectrum(own)

    my_tile = pl.ds(pl.multiple_of((my_line + 1) * OWN, OWN), OWN)

    @pl.loop(1, LINES)
    def _(step):
        target = (me + step) % LINES
        pltpu.make_async_remote_copy(
            src_ref=send2.at[pl.ds(pl.multiple_of(target * OWN, OWN), OWN), :],
            dst_ref=recv2.at[my_tile, :],
            send_sem=send_sem.at[1],
            recv_sem=recv_sem.at[1 + is_edge],
            device_id=(target, slab),
            device_id_type=MESH,
        ).start()

    recv2[my_tile, :] = send2[pl.ds(pl.multiple_of(me * OWN, OWN), OWN), :]
    outside = pl.ds(pl.multiple_of(slab * (LINES + 1) * OWN, OWN), OWN)
    recv2[outside, :] = jnp.zeros((OWN, LANES), F32)

    edge_tile = pl.ds(pl.multiple_of((LINES - slab * (LINES - 1)) * OWN, OWN), OWN)

    @pl.when(is_edge == 0)
    def _():
        one = pl.ds(0, OWN)
        pltpu.make_async_copy(recv2.at[one, :], recv2.at[one, :], recv_sem.at[2]).wait()

    beyond = pltpu.make_async_remote_copy(
        src_ref=recv2.at[edge_tile, :],
        dst_ref=recv2.at[outside, :],
        send_sem=edge_send,
        recv_sem=edge_recv,
        device_id=(me, 1 - slab),
        device_id_type=MESH,
    )
    beyond.start()

    @pl.when(is_edge == 1)
    def _():
        pltpu.make_async_copy(recv2.at[rest, :], recv2.at[rest, :], recv_sem.at[1]).wait()

    @pl.when(is_edge == 0)
    def _():
        less = pl.ds(0, (LINES - 2) * OWN)
        pltpu.make_async_copy(recv2.at[less, :], recv2.at[less, :], recv_sem.at[1]).wait()

    beyond.wait()

    @pl.loop(0, OWN)
    def _(own):
        flags = send1[pl.ds(own, LINES, stride=OWN), :][:, MASK_LANE : MASK_LANE + 1]
        keep = jnp.where(lane == 0, 1.0, 1.0 - jnp.broadcast_to(flags, (LINES, LANES)))
        f = finish(
            recv2[pl.ds(OWN + own, LINES, stride=OWN), :],
            recv2[pl.ds(2 * OWN + own, LINES, stride=OWN), :],
            recv2[pl.ds(own, LINES, stride=OWN), :],
            cross[1],
            keep,
        )
        out_ref[pl.ds(own, MOMENTS, stride=OWN), :] = f.T[:MOMENTS]

    @pl.loop(0, OWN)
    def _(own):
        near(own, 0).wait_send()
        near(own, 1).wait_send()

    pltpu.make_async_copy(send1.at[rest, :], send1.at[rest, :], send_sem.at[0]).wait()
    pltpu.make_async_copy(send2.at[rest, :], send2.at[rest, :], send_sem.at[1]).wait()


def local(moments, mask, coefficients, rates):
    t = tables()
    names = ["to_modes", "forward", "inverse", "series", "cross", "band", "rows", "pick", "modes_right"]
    constants = [jnp.asarray(t[name]) for name in names]
    in_vmem = pl.BlockSpec(memory_space=pltpu.VMEM)
    anywhere = pl.BlockSpec(memory_space=pl.ANY)
    tile = (NX, LANES)
    line = (OWN, LINES, LANES)
    out = pl.pallas_call(
        kernel,
        out_shape=jax.ShapeDtypeStruct((MOMENTS * OWN, LINES), F32),
        in_specs=[in_vmem] * 4 + [anywhere] * len(constants),
        out_specs=in_vmem,
        scratch_shapes=[pltpu.VMEM(c.shape, c.dtype) for c in constants]
        + [pltpu.VMEM(shape, F32) for shape in (tile, tile, tile, (NX + 2 * OWN, LANES), line, (2, *line), line, (OWN, 2 * HALF, LANES), (LANES, LANES), (1, LANES))]
        + [
            pltpu.VMEM((2 * LANES, 2 * LANES), BF16),
            pltpu.SemaphoreType.DMA((10,)),
            pltpu.SemaphoreType.DMA((2,)),
            pltpu.SemaphoreType.DMA((3,)),
            pltpu.SemaphoreType.DMA,
            pltpu.SemaphoreType.DMA,
            pltpu.SemaphoreType.DMA((2, OWN)),
            pltpu.SemaphoreType.DMA((2, OWN)),
        ],
        compiler_params=pltpu.CompilerParams(collective_id=0, has_side_effects=True, vmem_limit_bytes=48 * 1024 * 1024),
        name="duct",
    )(
        moments.reshape(MOMENTS * OWN, LINES),
        mask,
        coefficients,
        rates.reshape(1, MOMENTS),
        *constants,
    )
    return out.reshape(MOMENTS, OWN, LINES)


def solution(mesh):
    in_specs = (P(None, "wa", "gy"), P("wa", "gy"), P(), P())
    return jax.shard_map(local, mesh=mesh, in_specs=in_specs, out_specs=P(None, "wa", "gy"), check_vma=False)
```

```python
import functools
import math

import jax
import jax.numpy as jnp
import ml_dtypes
import numpy as np
from jax import lax
from jax.experimental import pallas as pl
from jax.experimental.pallas import tpu as pltpu
from jax.sharding import PartitionSpec as P

DEG = 7
AXIAL_STEP = 0.2
CROSS_STEP = 0.2
COLLIDE_STEP = 0.5
NX = 1024
LINES = 128
OWN = 8
LANES = 128
STRIDE = 37
MOMENTS = 120
MASK_LANE = 120
HALF = 72
BLOCKS = HALF // 8
ROOT_HALF = math.sqrt(0.5)

F32 = jnp.float32
BF16 = jnp.bfloat16
MESH = pl.DeviceIdType.MESH


def moment_table():
    entries = []
    for degree in range(DEG + 1):
        for k1 in range(degree, -1, -1):
            for k2 in range(degree - k1, -1, -1):
                entries.append((k1, k2, degree - k1 - k2))
    return entries


def hermite(order, point):
    previous, current = 0.0, 1.0
    for level in range(order):
        previous, current = current, point * current - level * previous
    return current


def hermite_roots(order):
    roots, step = [], 1.0 / 128
    low = -(2.0 * math.sqrt(order) + 1.0) - step / 3
    while len(roots) < order:
        high = low + step
        if (hermite(order, low) > 0) != (hermite(order, high) > 0):
            a, b = low, high
            for _ in range(80):
                middle = 0.5 * (a + b)
                if (hermite(order, middle) > 0) == (hermite(order, a) > 0):
                    a = middle
                else:
                    b = middle
            roots.append(0.5 * (a + b))
        low = high
    return roots


SPEED = hermite_roots(DEG + 1)[-1]


def coupling(entries, lookup, direction):
    matrix = np.zeros((LANES, LANES))
    for position, moment in enumerate(entries):
        raised = list(moment)
        raised[direction] += 1
        partner = lookup.get(tuple(raised))
        if partner is not None:
            matrix[position, partner] = matrix[partner, position] = math.sqrt(raised[direction])
    return matrix


def axial_modes(lookup):
    values = np.zeros(LANES)
    vectors = np.zeros((LANES, LANES))
    column = 0
    for k2 in range(DEG + 1):
        for k3 in range(DEG + 1 - k2):
            size = DEG + 1 - k2 - k3
            for root in hermite_roots(size):
                entry = [hermite(k, root) / math.sqrt(math.factorial(k)) for k in range(size)]
                norm = math.sqrt(sum(v * v for v in entry))
                for k in range(size):
                    vectors[lookup[k, k2, k3], column] = entry[k] / norm
                values[column] = root
                column += 1
    return values, vectors


def parts(table):
    high = table.astype(np.float32).astype(ml_dtypes.bfloat16)
    low = (table - high.astype(np.float64)).astype(np.float32).astype(ml_dtypes.bfloat16)
    return high, low


def right_factor(table):
    high, low = parts(table)
    return np.block([[high, low], [high, low]])


@functools.cache
def tables():
    entries = moment_table()
    lookup = {moment: position for position, moment in enumerate(entries)}
    values, modes = axial_modes(lookup)
    a2 = coupling(entries, lookup, 1)
    eye = np.eye(LANES)

    high, low = parts(modes.T)
    to_modes = np.concatenate([high, high, low], axis=1)

    k1 = np.arange(HALF)
    used = k1 <= 64
    weight = np.where(used, np.where((k1 == 0) | (k1 == 64), 1.0, 2.0), 0.0) / NX
    line = np.arange(LINES)
    forward, inverse = [], []
    for own in range(OWN):
        phase = (((OWN * line + own)[:, None] * k1[None, :]) % NX) * (2 * math.pi / NX)
        cosine, sine = np.cos(phase) * used, np.sin(phase) * used
        forward.append(np.concatenate(parts(np.concatenate([cosine.T, -sine.T], axis=0)), axis=0))
        inverse.append(np.concatenate(parts(np.concatenate([cosine * weight, -sine * weight], axis=1)), axis=0))
    forward, inverse = np.stack(forward), np.stack(inverse)

    wave = k1[None, :] + 128 * np.arange(8)[:, None]
    wave = np.where(wave < NX // 2, wave, wave - NX) * (AXIAL_STEP * 2 * math.pi / NX)
    angle = (wave[:, :, None] * values) * used[None, :, None]
    series = np.stack([1 - angle**2 / 2 + angle**4 / 24, -(angle - angle**3 / 6)])
    series = series.astype(np.float32)

    units = [lookup[1, 0, 0], lookup[0, 1, 0], lookup[0, 0, 1]]
    combinations = [(0,), (1,), (2,), (0, 1), (0, 2), (1, 2)]
    spare, target = eye.copy(), np.zeros((LANES, LANES))
    for lane, group in enumerate(combinations, MOMENTS):
        for d in group:
            spare[units[d], lane] = 1.0
    spare[MOMENTS:, MOMENTS:] = 0.0
    for position, moment in enumerate(entries):
        if sum(moment) == 2:
            d = tuple(direction for direction in range(3) for _ in range(moment[direction]))
            if d[0] == d[1]:
                target[MOMENTS + d[0], position] = COLLIDE_STEP * ROOT_HALF
            else:
                target[MOMENTS + combinations.index(d), position] = 0.5 * COLLIDE_STEP
                target[MOMENTS + d[0], position] = target[MOMENTS + d[1], position] = -0.5 * COLLIDE_STEP
    cross = np.concatenate([right_factor(modes.T @ spare), right_factor(modes.T @ (-0.5 * CROSS_STEP * a2) @ spare)])

    degrees = np.array([sum(moment) for moment in entries] + [0] * (LANES - MOMENTS))
    band = (np.abs(degrees[:, None] - degrees[None, :]) <= 1) & (degrees[:, None] >= 2) & (degrees[None, :] >= 2)
    band = (band * COLLIDE_STEP).astype(np.float32)
    target = target.astype(np.float32)
    relaxed = np.diag(COLLIDE_STEP * (degrees >= 2)).astype(np.float32)
    square = np.stack([band, target - relaxed, np.diag(np.arange(LANES) < MOMENTS).astype(np.float32)])
    high, low = parts(modes)
    modes_right = np.concatenate([high, high, low], axis=0)
    return dict(
        to_modes=to_modes, forward=forward, inverse=inverse, series=series, cross=cross, square=square, modes_right=modes_right,
    )


def doubled(a):
    high, low = split(a)
    both = jnp.concatenate([high, low], axis=1)
    return jnp.concatenate([both, both], axis=0)


def split(a):
    high = a.astype(BF16)
    return high, (a - high.astype(F32)).astype(BF16)


def fold(a):
    return a[:, :LANES] + a[:, LANES:]


def add(a, b):
    return (a[0] + b[0], a[1] + b[1])


def sub(a, b):
    return (a[0] - b[0], a[1] - b[1])


def quarter(a, sign):
    return (-a[1], a[0]) if sign > 0 else (a[1], -a[0])


def fourier4(v, sign):
    s, d = add(v[0], v[2]), sub(v[0], v[2])
    t, e = add(v[1], v[3]), quarter(sub(v[1], v[3]), sign)
    return [add(s, t), add(d, e), sub(s, t), sub(d, e)]


def fourier8(v, sign):
    even, odd = fourier4(v[0::2], sign), fourier4(v[1::2], sign)
    turned = [
        odd[0],
        ((odd[1][0] - sign * odd[1][1]) * ROOT_HALF, (odd[1][1] + sign * odd[1][0]) * ROOT_HALF),
        quarter(odd[2], sign),
        ((-odd[3][0] - sign * odd[3][1]) * ROOT_HALF, (-odd[3][1] + sign * odd[3][0]) * ROOT_HALF),
    ]
    return [add(a, b) for a, b in zip(even, turned)] + [sub(a, b) for a, b in zip(even, turned)]


def device_at(place):
    chip, core = place // 2, place % 2
    x_hi = chip // 32
    turn = chip % 32
    turn = turn + x_hi * (31 - 2 * turn)
    z = turn // 4
    y = turn % 4
    y = y + (z % 2) * (3 - 2 * y)
    return ((z * 2 + x_hi) * 4 + y) * 2 + core


def place_of(device):
    core, y, x_hi, z = device & 1, (device >> 1) & 3, (device >> 3) & 1, device >> 4
    turn = z * 4 + y + (z & 1) * (3 - 2 * y)
    return (x_hi * 32 + turn + x_hi * (31 - 2 * turn)) * 2 + core


def kernel(
    x_h, mask_h, c_h, rate_h,
    to_modes_h, forward_h, inverse_h, series_h, cross_h, square_h, modes_h,
    out_ref,
    x_ref, mask_ref, c_ref, rate_ref, to_modes, forward, inverse, series, cross, square, modes,
    send1, recv1, send2, recv2, lines, beside, wall, spectrum, padded, rate_row, collide, advance_modes,
    table_sem, send_sem, recv_sem, edge_send, edge_recv, near_send, near_recv,
):
    me, slab = lax.axis_index("wa"), lax.axis_index("gy")
    place = place_of(me)
    my_line = place + slab * (LINES - 1 - 2 * place)
    is_edge = place // (LINES - 1)
    next_wa, next_gy = device_at(place + 1 - is_edge), slab + is_edge * (1 - 2 * slab)
    is_first = 1 - (place + LINES - 1) // LINES
    prev_wa, prev_gy = device_at(place - 1 + is_first), slab + is_first * (1 - 2 * slab)

    loads = [
        pltpu.make_async_copy(src, dst, table_sem.at[i])
        for i, (src, dst) in enumerate(
            [(x_h, x_ref), (mask_h, mask_ref), (to_modes_h, to_modes), (c_h, c_ref), (rate_h, rate_ref), (forward_h, forward),
             (series_h, series), (inverse_h, inverse), (cross_h, cross), (square_h, square), (modes_h, modes)]
        )
    ]
    for load in loads[:3]:
        load.start()

    barrier = pltpu.get_barrier_semaphore()

    @pl.loop(1, LINES)
    def _(step):
        pl.semaphore_signal(barrier, inc=1, device_id=((me + step) & (LINES - 1), slab), device_id_type=MESH)

    pl.semaphore_signal(barrier, inc=1, device_id=(me, 1 - slab), device_id_type=MESH)

    for load in loads[3:]:
        load.start()
    for load in loads[:3]:
        load.wait()

    row = lax.broadcasted_iota(jnp.int32, (LANES, LANES), 0)
    lane = lax.broadcasted_iota(jnp.int32, (LANES, LANES), 1)

    @pl.loop(0, OWN, unroll=True)
    def _(own):
        cells = x_ref[pl.ds(own, MOMENTS, stride=OWN), :]
        cells = jnp.concatenate([cells, jnp.zeros((LANES - MOMENTS, LANES), F32)], axis=0)
        high, low = split(cells)
        turned = jnp.dot(to_modes[...], jnp.concatenate([high, low, high], axis=0), preferred_element_type=F32)
        flags = mask_ref[pl.ds(own, 1), :].astype(F32)
        turned = jnp.where(row == MASK_LANE, flags, turned)
        send1[pl.ds(own, LINES, stride=OWN), :] = turned.T

    pl.semaphore_wait(barrier, LINES)

    @pl.loop(1, LINES)
    def _(step):
        target = (me + step * STRIDE) & (LINES - 1)
        target_place = place_of(target)
        target_line = target_place + slab * (LINES - 1 - 2 * target_place)
        pltpu.make_async_remote_copy(
            src_ref=send1.at[pl.ds(pl.multiple_of(target_line * OWN, OWN), OWN), :],
            dst_ref=recv1.at[pl.ds(pl.multiple_of(me * OWN, OWN), OWN), :],
            send_sem=send_sem.at[0],
            recv_sem=recv_sem.at[0],
            device_id=(target, slab),
            device_id_type=MESH,
        ).start()

    recv1[pl.ds(pl.multiple_of(me * OWN, OWN), OWN), :] = send1[pl.ds(pl.multiple_of(my_line * OWN, OWN), OWN), :]

    for load in loads[3:]:
        load.wait()
    padded[...] = jnp.zeros_like(padded)
    padded[:MOMENTS, :MOMENTS] = c_ref[...]
    rate_row[...] = jnp.zeros_like(rate_row)
    rate_row[:, :MOMENTS] = rate_ref[...]
    linear = (padded[...] * square[0]).T + square[1] * rate_row[...] + square[2]
    collide[...] = doubled(linear)
    high, low = split(linear)
    linear = jnp.dot(jnp.concatenate([high, low, high], axis=1), modes[...], preferred_element_type=F32)
    advance_modes[...] = doubled(linear)

    def finish(here, sums, differences, keep, factor):
        here = here * (1 - CROSS_STEP * SPEED) + sums * (0.5 * CROSS_STEP * SPEED)
        operand = jnp.concatenate([*split(here), *split(differences)], axis=1)
        f = fold(jnp.dot(operand, cross[...], preferred_element_type=F32)) * keep
        f = jnp.where(lax.broadcasted_iota(jnp.int32, f.shape, 1) >= MOMENTS, f * f, f)
        return fold(jnp.dot(jnp.concatenate(split(f), axis=1), factor[...], preferred_element_type=F32))

    def to_spectrum(own, cells):
        table = forward[own]
        both = jnp.dot(jnp.concatenate([table, table], axis=1), jnp.concatenate(split(cells), axis=0), preferred_element_type=F32)
        spectrum[own] = both[: 2 * HALF] + both[2 * HALF :]

    def advance():
        @pl.loop(0, BLOCKS)
        def _(block):
            at = pl.multiple_of(block * 8, 8)
            re, im = pl.ds(at, 8), pl.ds(pl.multiple_of(HALF + at, 8), 8)
            f = fourier8([(spectrum[own, re, :], spectrum[own, im, :]) for own in range(OWN)], -1)
            h = []
            for k, (fr, fi) in enumerate(f):
                pr, pi = series[0, k, re, :], series[1, k, re, :]
                h.append((pr * fr - pi * fi, pr * fi + pi * fr))
            for own, (ur, ui) in enumerate(fourier8(h, 1)):
                spectrum[own, re, :] = ur
                spectrum[own, im, :] = ui

    def from_spectrum(own):
        both = fold(jnp.dot(inverse[own], jnp.concatenate(split(spectrum[own]), axis=1), preferred_element_type=F32))
        return both[:LINES] + both[LINES:]

    rest = pl.ds(0, (LINES - 1) * OWN)
    pltpu.make_async_copy(recv1.at[rest, :], recv1.at[rest, :], recv_sem.at[0]).wait()

    @pl.loop(0, OWN, unroll=True)
    def _(own):
        cells = recv1[pl.ds(own, LINES, stride=OWN), :]
        flags = jnp.broadcast_to(cells[:, MASK_LANE : MASK_LANE + 1], (LINES, LANES))
        wall[own] = jnp.where(lane == 0, 1.0, 1.0 - flags)
        to_spectrum(own, cells)

    advance()

    def near(own, which):
        slot = 1 - is_first if which else is_edge
        return pltpu.make_async_remote_copy(
            src_ref=lines.at[own],
            dst_ref=beside.at[slot, own],
            send_sem=near_send.at[which, own],
            recv_sem=near_recv.at[slot, own],
            device_id=(prev_wa, prev_gy) if which else (next_wa, next_gy),
            device_id_type=MESH,
        )

    @pl.loop(0, OWN, unroll=True)
    def _(own):
        lines[own] = from_spectrum(own)
        near(own, 0).start()
        near(own, 1).start()

    inside = 1.0 - is_first.astype(F32)
    upward = 1.0 - 2.0 * slab.astype(F32)

    @pl.loop(0, OWN, unroll=True)
    def _(own):
        for slot in range(2):
            pltpu.make_async_copy(lines.at[own], beside.at[slot, own], near_recv.at[slot, own]).wait()
        after, before = beside[1, own], beside[0, own] * inside
        to_spectrum(own, finish(lines[own], after + before, (after - before) * upward, wall[own], advance_modes))

    advance()

    @pl.loop(0, OWN, unroll=True)
    def _(own):
        send2[pl.ds(own, LINES, stride=OWN), :] = from_spectrum(own)

    my_tile = pl.ds(pl.multiple_of((my_line + 1) * OWN, OWN), OWN)

    @pl.loop(1, LINES)
    def _(step):
        target = (me + step * STRIDE) & (LINES - 1)
        pltpu.make_async_remote_copy(
            src_ref=send2.at[pl.ds(pl.multiple_of(target * OWN, OWN), OWN), :],
            dst_ref=recv2.at[my_tile, :],
            send_sem=send_sem.at[1],
            recv_sem=recv_sem.at[1 + is_edge],
            device_id=(target, slab),
            device_id_type=MESH,
        ).start()

    recv2[my_tile, :] = send2[pl.ds(pl.multiple_of(me * OWN, OWN), OWN), :]
    outside = pl.ds(pl.multiple_of(slab * (LINES + 1) * OWN, OWN), OWN)
    recv2[outside, :] = jnp.zeros((OWN, LANES), F32)

    edge_tile = pl.ds(pl.multiple_of((LINES - slab * (LINES - 1)) * OWN, OWN), OWN)

    @pl.when(is_edge == 0)
    def _():
        one = pl.ds(0, OWN)
        pltpu.make_async_copy(recv2.at[one, :], recv2.at[one, :], recv_sem.at[2]).wait()

    beyond = pltpu.make_async_remote_copy(
        src_ref=recv2.at[edge_tile, :],
        dst_ref=recv2.at[outside, :],
        send_sem=edge_send,
        recv_sem=edge_recv,
        device_id=(me, 1 - slab),
        device_id_type=MESH,
    )
    beyond.start()

    @pl.when(is_edge == 1)
    def _():
        pltpu.make_async_copy(recv2.at[rest, :], recv2.at[rest, :], recv_sem.at[1]).wait()

    @pl.when(is_edge == 0)
    def _():
        less = pl.ds(0, (LINES - 2) * OWN)
        pltpu.make_async_copy(recv2.at[less, :], recv2.at[less, :], recv_sem.at[1]).wait()

    beyond.wait()

    @pl.loop(0, OWN, unroll=True)
    def _(own):
        flags = send1[pl.ds(own, LINES, stride=OWN), :][:, MASK_LANE : MASK_LANE + 1]
        keep = jnp.where(lane == 0, 1.0, 1.0 - jnp.broadcast_to(flags, (LINES, LANES)))
        here = recv2[pl.ds(OWN + own, LINES, stride=OWN), :]
        after = recv2[pl.ds(2 * OWN + own, LINES, stride=OWN), :]
        before = recv2[pl.ds(own, LINES, stride=OWN), :]
        f = finish(here, after + before, after - before, keep, collide)
        out_ref[pl.ds(own, MOMENTS, stride=OWN), :] = f.T[:MOMENTS]

    @pl.loop(0, OWN, unroll=True)
    def _(own):
        near(own, 0).wait_send()
        near(own, 1).wait_send()

    pltpu.make_async_copy(send1.at[rest, :], send1.at[rest, :], send_sem.at[0]).wait()
    pltpu.make_async_copy(send2.at[rest, :], send2.at[rest, :], send_sem.at[1]).wait()


def local(moments, mask, coefficients, rates):
    t = tables()
    names = ["to_modes", "forward", "inverse", "series", "cross", "square", "modes_right"]
    constants = [jnp.asarray(t[name]) for name in names]
    in_vmem = pl.BlockSpec(memory_space=pltpu.VMEM)
    in_hbm = pl.BlockSpec(memory_space=pltpu.HBM)
    tile = (NX, LANES)
    line = (OWN, LINES, LANES)
    out = pl.pallas_call(
        kernel,
        out_shape=jax.ShapeDtypeStruct((MOMENTS * OWN, LINES), F32),
        in_specs=[in_hbm] * (4 + len(constants)),
        out_specs=in_vmem,
        scratch_shapes=[
            pltpu.VMEM((MOMENTS * OWN, LINES), F32),
            pltpu.VMEM((OWN, LINES), jnp.int32),
            pltpu.VMEM((MOMENTS, MOMENTS), F32),
            pltpu.VMEM((1, MOMENTS), F32),
        ]
        + [pltpu.VMEM(c.shape, c.dtype) for c in constants]
        + [pltpu.VMEM(shape, F32) for shape in (tile, tile, tile, (NX + 2 * OWN, LANES), line, (2, *line), line, (OWN, 2 * HALF, LANES), (LANES, LANES), (1, LANES))]
        + [
            pltpu.VMEM((2 * LANES, 2 * LANES), BF16),
            pltpu.VMEM((2 * LANES, 2 * LANES), BF16),
            pltpu.SemaphoreType.DMA((11,)),
            pltpu.SemaphoreType.DMA((2,)),
            pltpu.SemaphoreType.DMA((3,)),
            pltpu.SemaphoreType.DMA,
            pltpu.SemaphoreType.DMA,
            pltpu.SemaphoreType.DMA((2, OWN)),
            pltpu.SemaphoreType.DMA((2, OWN)),
        ],
        compiler_params=pltpu.CompilerParams(collective_id=0, has_side_effects=True, vmem_limit_bytes=62 * 1024 * 1024),
        name="duct",
    )(
        moments.reshape(MOMENTS * OWN, LINES),
        mask,
        coefficients,
        rates.reshape(1, MOMENTS),
        *constants,
    )
    return out.reshape(MOMENTS, OWN, LINES)


def solution(mesh):
    in_specs = (P(None, "wa", "gy"), P("wa", "gy"), P(), P())
    return jax.shard_map(local, mesh=mesh, in_specs=in_specs, out_specs=P(None, "wa", "gy"), check_vma=False)
```

```python
import functools
import math

import jax
import jax.numpy as jnp
import ml_dtypes
import numpy as np
from jax import lax
from jax.experimental import pallas as pl
from jax.experimental.pallas import tpu as pltpu
from jax.sharding import PartitionSpec as P

DEG = 7
AXIAL_STEP = 0.2
CROSS_STEP = 0.2
COLLIDE_STEP = 0.5
NX = 1024
LINES = 128
OWN = 8
LANES = 128
DISTANCES = (1, 7, 2, 6, 3, 5, 4, 0)
PLANE = 16
STRIDE = 37
MOMENTS = 120
MASK_LANE = 120
HALF = 72
BLOCKS = HALF // 8
ROOT_HALF = math.sqrt(0.5)

F32 = jnp.float32
BF16 = jnp.bfloat16
MESH = pl.DeviceIdType.MESH


def moment_table():
    entries = []
    for degree in range(DEG + 1):
        for k1 in range(degree, -1, -1):
            for k2 in range(degree - k1, -1, -1):
                entries.append((k1, k2, degree - k1 - k2))
    return entries


def hermite(order, point):
    previous, current = 0.0, 1.0
    for level in range(order):
        previous, current = current, point * current - level * previous
    return current


def hermite_roots(order):
    roots, step = [], 1.0 / 128
    low = -(2.0 * math.sqrt(order) + 1.0) - step / 3
    while len(roots) < order:
        high = low + step
        if (hermite(order, low) > 0) != (hermite(order, high) > 0):
            a, b = low, high
            for _ in range(80):
                middle = 0.5 * (a + b)
                if (hermite(order, middle) > 0) == (hermite(order, a) > 0):
                    a = middle
                else:
                    b = middle
            roots.append(0.5 * (a + b))
        low = high
    return roots


SPEED = hermite_roots(DEG + 1)[-1]


def coupling(entries, lookup, direction):
    matrix = np.zeros((LANES, LANES))
    for position, moment in enumerate(entries):
        raised = list(moment)
        raised[direction] += 1
        partner = lookup.get(tuple(raised))
        if partner is not None:
            matrix[position, partner] = matrix[partner, position] = math.sqrt(raised[direction])
    return matrix


def axial_modes(lookup):
    values = np.zeros(LANES)
    vectors = np.zeros((LANES, LANES))
    column = 0
    for k2 in range(DEG + 1):
        for k3 in range(DEG + 1 - k2):
            size = DEG + 1 - k2 - k3
            for root in hermite_roots(size):
                entry = [hermite(k, root) / math.sqrt(math.factorial(k)) for k in range(size)]
                norm = math.sqrt(sum(v * v for v in entry))
                for k in range(size):
                    vectors[lookup[k, k2, k3], column] = entry[k] / norm
                values[column] = root
                column += 1
    return values, vectors


def parts(table):
    high = table.astype(np.float32).astype(ml_dtypes.bfloat16)
    low = (table - high.astype(np.float64)).astype(np.float32).astype(ml_dtypes.bfloat16)
    return high, low


def right_factor(table):
    high, low = parts(table)
    return np.block([[high, low], [high, low]])


@functools.cache
def tables():
    entries = moment_table()
    lookup = {moment: position for position, moment in enumerate(entries)}
    values, modes = axial_modes(lookup)
    a2 = coupling(entries, lookup, 1)
    eye = np.eye(LANES)

    high, low = parts(modes.T)
    to_modes = np.concatenate([high, high, low], axis=1)

    k1 = np.arange(HALF)
    used = k1 <= 64
    weight = np.where(used, np.where((k1 == 0) | (k1 == 64), 1.0, 2.0), 0.0) / NX
    line = np.arange(LINES)
    forward, inverse = [], []
    for own in range(OWN):
        phase = (((OWN * line + own)[:, None] * k1[None, :]) % NX) * (2 * math.pi / NX)
        cosine, sine = np.cos(phase) * used, np.sin(phase) * used
        forward.append(np.concatenate(parts(np.concatenate([cosine.T, -sine.T], axis=0)), axis=0))
        high, low = parts(np.concatenate([cosine * weight, -sine * weight], axis=1))
        inverse.append(np.concatenate([high, high, low], axis=1))
    forward, inverse = np.stack(forward), np.stack(inverse)

    wave = k1[None, :] + 128 * np.arange(8)[:, None]
    wave = np.where(wave < NX // 2, wave, wave - NX) * (AXIAL_STEP * 2 * math.pi / NX)
    angle = (wave[:, :, None] * values) * used[None, :, None]
    series = np.stack([1 - angle**2 / 2 + angle**4 / 24, -(angle - angle**3 / 6)])
    series = series.astype(np.float32)

    units = [lookup[1, 0, 0], lookup[0, 1, 0], lookup[0, 0, 1]]
    combinations = [(0,), (1,), (2,), (0, 1), (0, 2), (1, 2)]
    spare, target = eye.copy(), np.zeros((LANES, LANES))
    for lane, group in enumerate(combinations, MOMENTS):
        for d in group:
            spare[units[d], lane] = 1.0
    spare[MOMENTS:, MOMENTS:] = 0.0
    for position, moment in enumerate(entries):
        if sum(moment) == 2:
            d = tuple(direction for direction in range(3) for _ in range(moment[direction]))
            if d[0] == d[1]:
                target[MOMENTS + d[0], position] = COLLIDE_STEP * ROOT_HALF
            else:
                target[MOMENTS + combinations.index(d), position] = 0.5 * COLLIDE_STEP
                target[MOMENTS + d[0], position] = target[MOMENTS + d[1], position] = -0.5 * COLLIDE_STEP
    cross = np.concatenate([right_factor(modes.T @ spare), right_factor(modes.T @ (-0.5 * CROSS_STEP * a2) @ spare)])

    degrees = np.array([sum(moment) for moment in entries] + [0] * (LANES - MOMENTS))
    band = (np.abs(degrees[:, None] - degrees[None, :]) <= 1) & (degrees[:, None] >= 2) & (degrees[None, :] >= 2)
    band = (band * COLLIDE_STEP).astype(np.float32)
    target = target.astype(np.float32)
    relaxed = np.diag(COLLIDE_STEP * (degrees >= 2)).astype(np.float32)
    square = np.stack([band, target - relaxed, np.diag(np.arange(LANES) < MOMENTS).astype(np.float32)])
    high, low = parts(modes)
    modes_right = np.concatenate([high, high, low], axis=0)
    return dict(
        to_modes=to_modes, forward=forward, inverse=inverse, series=series, cross=cross, square=square, modes_right=modes_right,
    )


def doubled(a):
    high, low = split(a)
    both = jnp.concatenate([high, low], axis=1)
    return jnp.concatenate([both, both], axis=0)


def split(a):
    high = a.astype(BF16)
    return high, (a - high.astype(F32)).astype(BF16)


def fold(a):
    return a[:, :LANES] + a[:, LANES:]


def add(a, b):
    return (a[0] + b[0], a[1] + b[1])


def sub(a, b):
    return (a[0] - b[0], a[1] - b[1])


def quarter(a, sign):
    return (-a[1], a[0]) if sign > 0 else (a[1], -a[0])


def fourier4(v, sign):
    s, d = add(v[0], v[2]), sub(v[0], v[2])
    t, e = add(v[1], v[3]), quarter(sub(v[1], v[3]), sign)
    return [add(s, t), add(d, e), sub(s, t), sub(d, e)]


def fourier8(v, sign):
    even, odd = fourier4(v[0::2], sign), fourier4(v[1::2], sign)
    turned = [
        odd[0],
        ((odd[1][0] - sign * odd[1][1]) * ROOT_HALF, (odd[1][1] + sign * odd[1][0]) * ROOT_HALF),
        quarter(odd[2], sign),
        ((-odd[3][0] - sign * odd[3][1]) * ROOT_HALF, (-odd[3][1] + sign * odd[3][0]) * ROOT_HALF),
    ]
    return [add(a, b) for a, b in zip(even, turned)] + [sub(a, b) for a, b in zip(even, turned)]


def device_at(place):
    chip, core = place // 2, place % 2
    x_hi = chip // 32
    turn = chip % 32
    turn = turn + x_hi * (31 - 2 * turn)
    z = turn // 4
    y = turn % 4
    y = y + (z % 2) * (3 - 2 * y)
    return ((z * 2 + x_hi) * 4 + y) * 2 + core


def place_of(device):
    core, y, x_hi, z = device & 1, (device >> 1) & 3, (device >> 3) & 1, device >> 4
    turn = z * 4 + y + (z & 1) * (3 - 2 * y)
    return (x_hi * 32 + turn + x_hi * (31 - 2 * turn)) * 2 + core


def kernel(
    x_h, mask_h, c_h, rate_h,
    to_modes_h, forward_h, inverse_h, series_h, cross_h, square_h, modes_h,
    out_ref,
    x_ref, mask_ref, c_ref, rate_ref, to_modes, forward, inverse, series, cross, square, modes,
    send1, recv1, send2, recv2, beside, wall, pair, spectrum, padded, rate_row, collide, advance_modes,
    table_sem, send_sem, plane_recv, recv_sem, edge_send, edge_recv, near_send, near_recv,
):
    me, slab = lax.axis_index("wa"), lax.axis_index("gy")
    place = place_of(me)
    my_line = place + slab * (LINES - 1 - 2 * place)
    is_edge = place // (LINES - 1)
    next_wa, next_gy = device_at(place + 1 - is_edge), slab + is_edge * (1 - 2 * slab)
    is_first = 1 - (place + LINES - 1) // LINES
    prev_wa, prev_gy = device_at(place - 1 + is_first), slab + is_first * (1 - 2 * slab)

    loads = [
        pltpu.make_async_copy(src, dst, table_sem.at[i])
        for i, (src, dst) in enumerate(
            [(x_h, x_ref), (mask_h, mask_ref), (to_modes_h, to_modes), (c_h, c_ref), (rate_h, rate_ref), (forward_h, forward),
             (series_h, series), (inverse_h, inverse), (cross_h, cross), (square_h, square), (modes_h, modes)]
        )
    ]
    for load in loads[:3]:
        load.start()

    barrier = pltpu.get_barrier_semaphore()

    @pl.loop(1, LINES)
    def _(step):
        pl.semaphore_signal(barrier, inc=1, device_id=((me + step) & (LINES - 1), slab), device_id_type=MESH)

    pl.semaphore_signal(barrier, inc=1, device_id=(me, 1 - slab), device_id_type=MESH)

    for load in loads[3:]:
        load.start()
    for load in loads[:3]:
        load.wait()

    row = lax.broadcasted_iota(jnp.int32, (LANES, LANES), 0)
    lane = lax.broadcasted_iota(jnp.int32, (LANES, LANES), 1)

    @pl.loop(0, OWN, unroll=True)
    def _(own):
        cells = x_ref[pl.ds(own, MOMENTS, stride=OWN), :]
        cells = jnp.concatenate([cells, jnp.zeros((LANES - MOMENTS, LANES), F32)], axis=0)
        high, low = split(cells)
        turned = jnp.dot(to_modes[...], jnp.concatenate([high, low, high], axis=0), preferred_element_type=F32)
        flags = mask_ref[pl.ds(own, 1), :].astype(F32)
        turned = jnp.where(row == MASK_LANE, flags, turned)
        send1[pl.ds(own, LINES, stride=OWN), :] = turned.T

    pl.semaphore_wait(barrier, LINES)

    z = me >> 4

    for distance in DISTANCES:

        @pl.loop(0 if distance else 1, PLANE)
        def _(step):
            target = ((z + distance) & 7) * PLANE + ((me + step) & (PLANE - 1))
            target_place = place_of(target)
            target_line = target_place + slab * (LINES - 1 - 2 * target_place)
            pltpu.make_async_remote_copy(
                src_ref=send1.at[pl.ds(pl.multiple_of(target_line * OWN, OWN), OWN), :],
                dst_ref=recv1.at[pl.ds(pl.multiple_of(me * OWN, OWN), OWN), :],
                send_sem=send_sem.at[0],
                recv_sem=plane_recv.at[z],
                device_id=(target, slab),
                device_id_type=MESH,
            ).start()

    recv1[pl.ds(pl.multiple_of(me * OWN, OWN), OWN), :] = send1[pl.ds(pl.multiple_of(my_line * OWN, OWN), OWN), :]

    for load in loads[3:]:
        load.wait()
    padded[...] = jnp.zeros_like(padded)
    padded[:MOMENTS, :MOMENTS] = c_ref[...]
    rate_row[...] = jnp.zeros_like(rate_row)
    rate_row[:, :MOMENTS] = rate_ref[...]
    linear = (padded[...] * square[0]).T + square[1] * rate_row[...] + square[2]
    collide[...] = doubled(linear)
    high, low = split(linear)
    linear = jnp.dot(jnp.concatenate([high, low, high], axis=1), modes[...], preferred_element_type=F32)
    advance_modes[...] = doubled(linear)

    def beside_terms(here, after, before):
        return here * (1 - CROSS_STEP * SPEED) + (after + before) * (0.5 * CROSS_STEP * SPEED), after - before

    def finish(fields, keeps, factor):
        moved = []
        for (here, differences), keep in zip(fields, keeps):
            operand = jnp.concatenate([*split(here), *split(differences)], axis=1)
            moved.append(fold(jnp.dot(operand, cross[...], preferred_element_type=F32)) * keep())
        moved = [jnp.where(lane >= MOMENTS, f * f, f) for f in moved]
        return [fold(jnp.dot(jnp.concatenate(split(f), axis=1), factor[...], preferred_element_type=F32)) for f in moved]

    def to_spectrum(own, cells):
        table = forward[own]
        both = jnp.dot(jnp.concatenate([table, table], axis=1), jnp.concatenate(split(cells), axis=0), preferred_element_type=F32)
        return both[: 2 * HALF] + both[2 * HALF :]

    def advance(spectrum, start):
        lanes = pl.ds(start, LANES)

        @pl.loop(0, BLOCKS)
        def _(block):
            at = pl.multiple_of(block * 8, 8)
            re, im = pl.ds(at, 8), pl.ds(pl.multiple_of(HALF + at, 8), 8)
            f = fourier8([(spectrum[own, re, lanes], spectrum[own, im, lanes]) for own in range(OWN)], -1)
            h = []
            for k, (fr, fi) in enumerate(f):
                pr, pi = series[0, k, re, :], series[1, k, re, :]
                h.append((pr * fr - pi * fi, pr * fi + pi * fr))
            for own, (ur, ui) in enumerate(fourier8(h, 1)):
                spectrum[own, re, lanes] = ur
                spectrum[own, im, lanes] = ui

    def from_spectrum(own, values):
        high, low = split(values)
        return jnp.dot(inverse[own], jnp.concatenate([high, low, high], axis=0), preferred_element_type=F32)

    def near(plane, which):
        slot = 1 - is_first if which else is_edge
        part = pl.ds(pl.multiple_of(plane * (PLANE * OWN), PLANE * OWN), PLANE * OWN)
        return pltpu.make_async_remote_copy(
            src_ref=recv1.at[part, :],
            dst_ref=beside.at[slot, part, :],
            send_sem=near_send.at[which, plane],
            recv_sem=near_recv.at[slot, plane],
            device_id=(prev_wa, prev_gy) if which else (next_wa, next_gy),
            device_id_type=MESH,
        )

    for distance in DISTANCES:
        plane = (z - distance) & 7
        part = pl.ds(0, (PLANE if distance else PLANE - 1) * OWN)
        pltpu.make_async_copy(recv1.at[part, :], recv1.at[part, :], plane_recv.at[plane]).wait()
        near(plane, 0).start()
        near(plane, 1).start()

    @pl.loop(0, OWN)
    def _(plane):
        part = pl.ds(pl.multiple_of(plane * (PLANE * OWN), PLANE * OWN), PLANE * OWN)
        for slot in range(2):
            pltpu.make_async_copy(recv1.at[part, :], beside.at[slot, part, :], near_recv.at[slot, plane]).wait()

    inside = 1.0 - is_first.astype(F32)
    upward = 1.0 - 2.0 * slab.astype(F32)

    @pl.loop(0, OWN, unroll=True)
    def _(own):
        rows = pl.ds(own, LINES, stride=OWN)
        cells = recv1[rows, :]
        flags = jnp.broadcast_to(cells[:, MASK_LANE : MASK_LANE + 1], (LINES, LANES))
        wall[own] = jnp.where(lane == 0, 1.0, 1.0 - flags)
        here, differences = beside_terms(cells, beside[1, rows, :], beside[0, rows, :] * inside)
        pair[own] = to_spectrum(own, jnp.concatenate([here, differences * upward], axis=1))

    advance(pair, 0)
    advance(pair, LANES)

    fields = [from_spectrum(own, pair[own]) for own in range(OWN)]
    fields = [(f[:, :LANES], f[:, LANES:]) for f in fields]
    for own, f in enumerate(finish(fields, [functools.partial(wall.__getitem__, own) for own in range(OWN)], advance_modes)):
        spectrum[own] = to_spectrum(own, f)

    advance(spectrum, 0)

    @pl.loop(0, OWN, unroll=True)
    def _(own):
        send2[pl.ds(own, LINES, stride=OWN), :] = from_spectrum(own, spectrum[own])

    my_tile = pl.ds(pl.multiple_of((my_line + 1) * OWN, OWN), OWN)

    @pl.loop(1, LINES)
    def _(step):
        target = (me + step * STRIDE) & (LINES - 1)
        pltpu.make_async_remote_copy(
            src_ref=send2.at[pl.ds(pl.multiple_of(target * OWN, OWN), OWN), :],
            dst_ref=recv2.at[my_tile, :],
            send_sem=send_sem.at[1],
            recv_sem=recv_sem.at[is_edge],
            device_id=(target, slab),
            device_id_type=MESH,
        ).start()

    recv2[my_tile, :] = send2[pl.ds(pl.multiple_of(me * OWN, OWN), OWN), :]
    outside = pl.ds(pl.multiple_of(slab * (LINES + 1) * OWN, OWN), OWN)
    recv2[outside, :] = jnp.zeros((OWN, LANES), F32)

    edge_tile = pl.ds(pl.multiple_of((LINES - slab * (LINES - 1)) * OWN, OWN), OWN)

    rest = pl.ds(0, (LINES - 1) * OWN)

    @pl.when(is_edge == 0)
    def _():
        one = pl.ds(0, OWN)
        pltpu.make_async_copy(recv2.at[one, :], recv2.at[one, :], recv_sem.at[1]).wait()

    beyond = pltpu.make_async_remote_copy(
        src_ref=recv2.at[edge_tile, :],
        dst_ref=recv2.at[outside, :],
        send_sem=edge_send,
        recv_sem=edge_recv,
        device_id=(me, 1 - slab),
        device_id_type=MESH,
    )
    beyond.start()

    @pl.when(is_edge == 1)
    def _():
        pltpu.make_async_copy(recv2.at[rest, :], recv2.at[rest, :], recv_sem.at[0]).wait()

    @pl.when(is_edge == 0)
    def _():
        less = pl.ds(0, (LINES - 2) * OWN)
        pltpu.make_async_copy(recv2.at[less, :], recv2.at[less, :], recv_sem.at[0]).wait()

    beyond.wait()

    def keep_here(own):
        flags = send1[pl.ds(own, LINES, stride=OWN), :][:, MASK_LANE : MASK_LANE + 1]
        return jnp.where(lane == 0, 1.0, 1.0 - jnp.broadcast_to(flags, (LINES, LANES)))

    fields = []
    for own in range(OWN):
        before, here, after = (recv2[pl.ds(tile * OWN + own, LINES, stride=OWN), :] for tile in range(3))
        fields.append(beside_terms(here, after, before))
    for own, f in enumerate(finish(fields, [functools.partial(keep_here, own) for own in range(OWN)], collide)):
        out_ref[pl.ds(own, MOMENTS, stride=OWN), :] = f.T[:MOMENTS]

    @pl.loop(0, OWN)
    def _(plane):
        near(plane, 0).wait_send()
        near(plane, 1).wait_send()

    pltpu.make_async_copy(send1.at[rest, :], send1.at[rest, :], send_sem.at[0]).wait()
    pltpu.make_async_copy(send2.at[rest, :], send2.at[rest, :], send_sem.at[1]).wait()


def local(moments, mask, coefficients, rates):
    t = tables()
    names = ["to_modes", "forward", "inverse", "series", "cross", "square", "modes_right"]
    constants = [jnp.asarray(t[name]) for name in names]
    in_vmem = pl.BlockSpec(memory_space=pltpu.VMEM)
    in_hbm = pl.BlockSpec(memory_space=pltpu.HBM)
    tile = (NX, LANES)
    line = (OWN, LINES, LANES)
    out = pl.pallas_call(
        kernel,
        out_shape=jax.ShapeDtypeStruct((MOMENTS * OWN, LINES), F32),
        in_specs=[in_hbm] * (4 + len(constants)),
        out_specs=in_vmem,
        scratch_shapes=[
            pltpu.VMEM((MOMENTS * OWN, LINES), F32),
            pltpu.VMEM((OWN, LINES), jnp.int32),
            pltpu.VMEM((MOMENTS, MOMENTS), F32),
            pltpu.VMEM((1, MOMENTS), F32),
        ]
        + [pltpu.VMEM(c.shape, c.dtype) for c in constants]
        + [pltpu.VMEM(shape, F32) for shape in (
            tile, tile, tile, (NX + 2 * OWN, LANES), (2, *tile), line, (OWN, 2 * HALF, 2 * LANES), (OWN, 2 * HALF, LANES),
            (LANES, LANES), (1, LANES),
        )]
        + [
            pltpu.VMEM((2 * LANES, 2 * LANES), BF16),
            pltpu.VMEM((2 * LANES, 2 * LANES), BF16),
            pltpu.SemaphoreType.DMA((11,)),
            pltpu.SemaphoreType.DMA((2,)),
            pltpu.SemaphoreType.DMA((8,)),
            pltpu.SemaphoreType.DMA((2,)),
            pltpu.SemaphoreType.DMA,
            pltpu.SemaphoreType.DMA,
            pltpu.SemaphoreType.DMA((2, OWN)),
            pltpu.SemaphoreType.DMA((2, OWN)),
        ],
        compiler_params=pltpu.CompilerParams(collective_id=0, has_side_effects=True, vmem_limit_bytes=62 * 1024 * 1024),
        name="duct",
    )(
        moments.reshape(MOMENTS * OWN, LINES),
        mask,
        coefficients,
        rates.reshape(1, MOMENTS),
        *constants,
    )
    return out.reshape(MOMENTS, OWN, LINES)


def solution(mesh):
    in_specs = (P(None, "wa", "gy"), P("wa", "gy"), P(), P())
    return jax.shard_map(local, mesh=mesh, in_specs=in_specs, out_specs=P(None, "wa", "gy"), check_vma=False)
```

```python
import functools
import math

import jax
import jax.numpy as jnp
import ml_dtypes
import numpy as np
from jax import lax
from jax.experimental import pallas as pl
from jax.experimental.pallas import tpu as pltpu
from jax.sharding import PartitionSpec as P

DEG = 7
AXIAL_STEP = 0.2
CROSS_STEP = 0.2
COLLIDE_STEP = 0.5
NX = 1024
LINES = 128
OWN = 8
LANES = 128
DISTANCES = (4, 0, 3, 5, 2, 6, 1, 7)
PLANE = 16
STRIDE = 37
MOMENTS = 120
MASK_LANE = 120
HALF = 72
BLOCKS = HALF // 8
ROOT_HALF = math.sqrt(0.5)

F32 = jnp.float32
BF16 = jnp.bfloat16
MESH = pl.DeviceIdType.MESH


def moment_table():
    entries = []
    for degree in range(DEG + 1):
        for k1 in range(degree, -1, -1):
            for k2 in range(degree - k1, -1, -1):
                entries.append((k1, k2, degree - k1 - k2))
    return entries


def hermite(order, point):
    previous, current = 0.0, 1.0
    for level in range(order):
        previous, current = current, point * current - level * previous
    return current


def hermite_roots(order):
    roots, step = [], 1.0 / 128
    low = -(2.0 * math.sqrt(order) + 1.0) - step / 3
    while len(roots) < order:
        high = low + step
        if (hermite(order, low) > 0) != (hermite(order, high) > 0):
            a, b = low, high
            for _ in range(80):
                middle = 0.5 * (a + b)
                if (hermite(order, middle) > 0) == (hermite(order, a) > 0):
                    a = middle
                else:
                    b = middle
            roots.append(0.5 * (a + b))
        low = high
    return roots


SPEED = hermite_roots(DEG + 1)[-1]


def coupling(entries, lookup, direction):
    matrix = np.zeros((LANES, LANES))
    for position, moment in enumerate(entries):
        raised = list(moment)
        raised[direction] += 1
        partner = lookup.get(tuple(raised))
        if partner is not None:
            matrix[position, partner] = matrix[partner, position] = math.sqrt(raised[direction])
    return matrix


def axial_modes(lookup):
    values = np.zeros(LANES)
    vectors = np.zeros((LANES, LANES))
    column = 0
    for k2 in range(DEG + 1):
        for k3 in range(DEG + 1 - k2):
            size = DEG + 1 - k2 - k3
            for root in hermite_roots(size):
                entry = [hermite(k, root) / math.sqrt(math.factorial(k)) for k in range(size)]
                norm = math.sqrt(sum(v * v for v in entry))
                for k in range(size):
                    vectors[lookup[k, k2, k3], column] = entry[k] / norm
                values[column] = root
                column += 1
    return values, vectors


def parts(table):
    high = table.astype(np.float32).astype(ml_dtypes.bfloat16)
    low = (table - high.astype(np.float64)).astype(np.float32).astype(ml_dtypes.bfloat16)
    return high, low


def right_factor(table):
    high, low = parts(table)
    return np.block([[high, low], [high, low]])


@functools.cache
def tables():
    entries = moment_table()
    lookup = {moment: position for position, moment in enumerate(entries)}
    values, modes = axial_modes(lookup)
    a2 = coupling(entries, lookup, 1)
    eye = np.eye(LANES)

    high, low = parts(modes.T)
    to_modes = np.concatenate([high, high, low], axis=1)

    k1 = np.arange(HALF)
    used = k1 <= 64
    weight = np.where(used, np.where((k1 == 0) | (k1 == 64), 1.0, 2.0), 0.0) / NX
    line = np.arange(LINES)
    forward, inverse = [], []
    for own in range(OWN):
        phase = (((OWN * line + own)[:, None] * k1[None, :]) % NX) * (2 * math.pi / NX)
        cosine, sine = np.cos(phase) * used, np.sin(phase) * used
        forward.append(np.concatenate(parts(np.concatenate([cosine.T, -sine.T], axis=0)), axis=0))
        high, low = parts(np.concatenate([cosine * weight, -sine * weight], axis=1))
        inverse.append(np.concatenate([high, high, low], axis=1))
    forward, inverse = np.stack(forward), np.stack(inverse)

    wave = k1[None, :] + 128 * np.arange(8)[:, None]
    wave = np.where(wave < NX // 2, wave, wave - NX) * (AXIAL_STEP * 2 * math.pi / NX)
    angle = (wave[:, :, None] * values) * used[None, :, None]
    series = np.stack([1 - angle**2 / 2 + angle**4 / 24, -(angle - angle**3 / 6)])
    series = series.astype(np.float32)

    units = [lookup[1, 0, 0], lookup[0, 1, 0], lookup[0, 0, 1]]
    combinations = [(0,), (1,), (2,), (0, 1), (0, 2), (1, 2)]
    spare, target = eye.copy(), np.zeros((LANES, LANES))
    for lane, group in enumerate(combinations, MOMENTS):
        for d in group:
            spare[units[d], lane] = 1.0
    spare[MOMENTS:, MOMENTS:] = 0.0
    for position, moment in enumerate(entries):
        if sum(moment) == 2:
            d = tuple(direction for direction in range(3) for _ in range(moment[direction]))
            if d[0] == d[1]:
                target[MOMENTS + d[0], position] = COLLIDE_STEP * ROOT_HALF
            else:
                target[MOMENTS + combinations.index(d), position] = 0.5 * COLLIDE_STEP
                target[MOMENTS + d[0], position] = target[MOMENTS + d[1], position] = -0.5 * COLLIDE_STEP
    cross = np.concatenate([right_factor(modes.T @ spare), right_factor(modes.T @ (-0.5 * CROSS_STEP * a2) @ spare)])

    degrees = np.array([sum(moment) for moment in entries] + [0] * (LANES - MOMENTS))
    band = (np.abs(degrees[:, None] - degrees[None, :]) <= 1) & (degrees[:, None] >= 2) & (degrees[None, :] >= 2)
    band = (band * COLLIDE_STEP).astype(np.float32)
    target = target.astype(np.float32)
    relaxed = np.diag(COLLIDE_STEP * (degrees >= 2)).astype(np.float32)
    square = np.stack([band, target - relaxed, np.diag(np.arange(LANES) < MOMENTS).astype(np.float32)])
    high, low = parts(modes)
    modes_right = np.concatenate([high, high, low], axis=0)
    return dict(
        to_modes=to_modes, forward=forward, inverse=inverse, series=series, cross=cross, square=square, modes_right=modes_right,
    )


def doubled(a):
    high, low = split(a)
    both = jnp.concatenate([high, low], axis=1)
    return jnp.concatenate([both, both], axis=0)


def split(a):
    high = a.astype(BF16)
    return high, (a - high.astype(F32)).astype(BF16)


def fold(a):
    return a[:, :LANES] + a[:, LANES:]


def add(a, b):
    return (a[0] + b[0], a[1] + b[1])


def sub(a, b):
    return (a[0] - b[0], a[1] - b[1])


def quarter(a, sign):
    return (-a[1], a[0]) if sign > 0 else (a[1], -a[0])


def fourier4(v, sign):
    s, d = add(v[0], v[2]), sub(v[0], v[2])
    t, e = add(v[1], v[3]), quarter(sub(v[1], v[3]), sign)
    return [add(s, t), add(d, e), sub(s, t), sub(d, e)]


def fourier8(v, sign):
    even, odd = fourier4(v[0::2], sign), fourier4(v[1::2], sign)
    turned = [
        odd[0],
        ((odd[1][0] - sign * odd[1][1]) * ROOT_HALF, (odd[1][1] + sign * odd[1][0]) * ROOT_HALF),
        quarter(odd[2], sign),
        ((-odd[3][0] - sign * odd[3][1]) * ROOT_HALF, (-odd[3][1] + sign * odd[3][0]) * ROOT_HALF),
    ]
    return [add(a, b) for a, b in zip(even, turned)] + [sub(a, b) for a, b in zip(even, turned)]


def device_at(place):
    chip, core = place // 2, place % 2
    x_hi = chip // 32
    turn = chip % 32
    turn = turn + x_hi * (31 - 2 * turn)
    z = turn // 4
    y = turn % 4
    y = y + (z % 2) * (3 - 2 * y)
    return ((z * 2 + x_hi) * 4 + y) * 2 + core


def place_of(device):
    core, y, x_hi, z = device & 1, (device >> 1) & 3, (device >> 3) & 1, device >> 4
    turn = z * 4 + y + (z & 1) * (3 - 2 * y)
    return (x_hi * 32 + turn + x_hi * (31 - 2 * turn)) * 2 + core


def kernel(
    x_h, mask_h, c_h, rate_h,
    to_modes_h, forward_h, inverse_h, series_h, cross_h, square_h, modes_h,
    out_ref,
    x_ref, mask_ref, c_ref, rate_ref, to_modes, forward, inverse, series, cross, square, modes,
    send1, recv1, send2, recv2, beside, wall, pair, spectrum, padded, rate_row, collide, advance_modes,
    table_sem, send_sem, plane_recv, recv_sem, edge_send, edge_recv, near_send, near_recv,
):
    me, slab = lax.axis_index("wa"), lax.axis_index("gy")
    place = place_of(me)
    my_line = place + slab * (LINES - 1 - 2 * place)
    is_edge = place // (LINES - 1)
    next_wa, next_gy = device_at(place + 1 - is_edge), slab + is_edge * (1 - 2 * slab)
    is_first = 1 - (place + LINES - 1) // LINES
    prev_wa, prev_gy = device_at(place - 1 + is_first), slab + is_first * (1 - 2 * slab)

    loads = [
        pltpu.make_async_copy(src, dst, table_sem.at[i])
        for i, (src, dst) in enumerate(
            [(x_h, x_ref), (mask_h, mask_ref), (to_modes_h, to_modes), (c_h, c_ref), (rate_h, rate_ref), (forward_h, forward),
             (series_h, series), (inverse_h, inverse), (cross_h, cross), (square_h, square), (modes_h, modes)]
        )
    ]
    for load in loads[:3]:
        load.start()

    barrier = pltpu.get_barrier_semaphore()

    @pl.loop(1, LINES, unroll=8)
    def _(step):
        pl.semaphore_signal(barrier, inc=1, device_id=((me + step) & (LINES - 1), slab), device_id_type=MESH)

    pl.semaphore_signal(barrier, inc=1, device_id=(me, 1 - slab), device_id_type=MESH)

    for load in loads[3:]:
        load.start()
    for load in loads[:3]:
        load.wait()

    row = lax.broadcasted_iota(jnp.int32, (LANES, LANES), 0)
    lane = lax.broadcasted_iota(jnp.int32, (LANES, LANES), 1)

    @pl.loop(0, OWN, unroll=True)
    def _(own):
        cells = x_ref[pl.ds(own, MOMENTS, stride=OWN), :]
        cells = jnp.concatenate([cells, jnp.zeros((LANES - MOMENTS, LANES), F32)], axis=0)
        high, low = split(cells)
        turned = jnp.dot(to_modes[...], jnp.concatenate([high, low, high], axis=0), preferred_element_type=F32)
        flags = mask_ref[pl.ds(own, 1), :].astype(F32)
        turned = jnp.where(row == MASK_LANE, flags, turned)
        send1[pl.ds(own, LINES, stride=OWN), :] = turned.T

    pl.semaphore_wait(barrier, LINES)

    z = me >> 4

    def serve1(target):
        target_place = place_of(target)
        target_line = target_place + slab * (LINES - 1 - 2 * target_place)
        pltpu.make_async_remote_copy(
            src_ref=send1.at[pl.ds(pl.multiple_of(target_line * OWN, OWN), OWN), :],
            dst_ref=recv1.at[pl.ds(pl.multiple_of(me * OWN, OWN), OWN), :],
            send_sem=send_sem.at[0],
            recv_sem=plane_recv.at[z],
            device_id=(target, slab),
            device_id_type=MESH,
        ).start()

    for first in range(0, 8, 2):
        pair_of = DISTANCES[first : first + 2]

        @pl.loop(0, PLANE)
        def _(step):
            for distance in pair_of:
                if distance:
                    serve1(((z + distance) & 7) * PLANE + ((me + step) & (PLANE - 1)))

        if 0 in pair_of:

            @pl.loop(1, PLANE)
            def _(step):
                serve1(z * PLANE + ((me + step) & (PLANE - 1)))

    recv1[pl.ds(pl.multiple_of(me * OWN, OWN), OWN), :] = send1[pl.ds(pl.multiple_of(my_line * OWN, OWN), OWN), :]

    for load in loads[3:]:
        load.wait()
    padded[...] = jnp.zeros_like(padded)
    padded[:MOMENTS, :MOMENTS] = c_ref[...]
    rate_row[...] = jnp.zeros_like(rate_row)
    rate_row[:, :MOMENTS] = rate_ref[...]
    linear = (padded[...] * square[0]).T + square[1] * rate_row[...] + square[2]
    collide[...] = doubled(linear)
    high, low = split(linear)
    linear = jnp.dot(jnp.concatenate([high, low, high], axis=1), modes[...], preferred_element_type=F32)
    advance_modes[...] = doubled(linear)

    def beside_terms(here, after, before):
        return here * (1 - CROSS_STEP * SPEED) + (after + before) * (0.5 * CROSS_STEP * SPEED), after - before

    def finish(fields, keeps, factor):
        moved = []
        for (here, differences), keep in zip(fields, keeps):
            operand = jnp.concatenate([*split(here), *split(differences)], axis=1)
            moved.append(fold(jnp.dot(operand, cross[...], preferred_element_type=F32)) * keep())
        moved = [jnp.where(lane >= MOMENTS, f * f, f) for f in moved]
        return [fold(jnp.dot(jnp.concatenate(split(f), axis=1), factor[...], preferred_element_type=F32)) for f in moved]

    def to_spectrum(own, cells):
        table = forward[own]
        both = jnp.dot(jnp.concatenate([table, table], axis=1), jnp.concatenate(split(cells), axis=0), preferred_element_type=F32)
        return both[: 2 * HALF] + both[2 * HALF :]

    def advance(spectrum, start):
        lanes = pl.ds(start, LANES)

        @pl.loop(0, BLOCKS)
        def _(block):
            at = pl.multiple_of(block * 8, 8)
            re, im = pl.ds(at, 8), pl.ds(pl.multiple_of(HALF + at, 8), 8)
            f = fourier8([(spectrum[own, re, lanes], spectrum[own, im, lanes]) for own in range(OWN)], -1)
            h = []
            for k, (fr, fi) in enumerate(f):
                pr, pi = series[0, k, re, :], series[1, k, re, :]
                h.append((pr * fr - pi * fi, pr * fi + pi * fr))
            for own, (ur, ui) in enumerate(fourier8(h, 1)):
                spectrum[own, re, lanes] = ur
                spectrum[own, im, lanes] = ui

    def from_spectrum(own, values):
        high, low = split(values)
        return jnp.dot(inverse[own], jnp.concatenate([high, low, high], axis=0), preferred_element_type=F32)

    def near(plane, which):
        slot = 1 - is_first if which else is_edge
        part = pl.ds(pl.multiple_of(plane * (PLANE * OWN), PLANE * OWN), PLANE * OWN)
        return pltpu.make_async_remote_copy(
            src_ref=recv1.at[part, :],
            dst_ref=beside.at[slot, part, :],
            send_sem=near_send.at[which, plane],
            recv_sem=near_recv.at[slot, plane],
            device_id=(prev_wa, prev_gy) if which else (next_wa, next_gy),
            device_id_type=MESH,
        )

    for distance in DISTANCES:
        plane = (z - distance) & 7
        part = pl.ds(0, (PLANE if distance else PLANE - 1) * OWN)
        pltpu.make_async_copy(recv1.at[part, :], recv1.at[part, :], plane_recv.at[plane]).wait()
        near(plane, 0).start()
        near(plane, 1).start()

    @pl.loop(0, OWN)
    def _(plane):
        part = pl.ds(pl.multiple_of(plane * (PLANE * OWN), PLANE * OWN), PLANE * OWN)
        for slot in range(2):
            pltpu.make_async_copy(recv1.at[part, :], beside.at[slot, part, :], near_recv.at[slot, plane]).wait()

    inside = 1.0 - is_first.astype(F32)
    upward = 1.0 - 2.0 * slab.astype(F32)

    @pl.loop(0, OWN, unroll=True)
    def _(own):
        rows = pl.ds(own, LINES, stride=OWN)
        cells = recv1[rows, :]
        flags = jnp.broadcast_to(cells[:, MASK_LANE : MASK_LANE + 1], (LINES, LANES))
        wall[own] = jnp.where(lane == 0, 1.0, 1.0 - flags)
        here, differences = beside_terms(cells, beside[1, rows, :], beside[0, rows, :] * inside)
        pair[own] = to_spectrum(own, jnp.concatenate([here, differences * upward], axis=1))

    advance(pair, 0)
    advance(pair, LANES)

    fields = [from_spectrum(own, pair[own]) for own in range(OWN)]
    fields = [(f[:, :LANES], f[:, LANES:]) for f in fields]
    for own, f in enumerate(finish(fields, [functools.partial(wall.__getitem__, own) for own in range(OWN)], advance_modes)):
        spectrum[own] = to_spectrum(own, f)

    advance(spectrum, 0)

    @pl.loop(0, OWN, unroll=True)
    def _(own):
        send2[pl.ds(own, LINES, stride=OWN), :] = from_spectrum(own, spectrum[own])

    my_tile = pl.ds(pl.multiple_of((my_line + 1) * OWN, OWN), OWN)

    @pl.loop(1, LINES)
    def _(step):
        target = (me + ((step + 1) >> 1) * (STRIDE * (2 * (step & 1) - 1))) & (LINES - 1)
        pltpu.make_async_remote_copy(
            src_ref=send2.at[pl.ds(pl.multiple_of(target * OWN, OWN), OWN), :],
            dst_ref=recv2.at[my_tile, :],
            send_sem=send_sem.at[1],
            recv_sem=recv_sem.at[is_edge],
            device_id=(target, slab),
            device_id_type=MESH,
        ).start()

    recv2[my_tile, :] = send2[pl.ds(pl.multiple_of(me * OWN, OWN), OWN), :]
    outside = pl.ds(pl.multiple_of(slab * (LINES + 1) * OWN, OWN), OWN)
    recv2[outside, :] = jnp.zeros((OWN, LANES), F32)

    edge_tile = pl.ds(pl.multiple_of((LINES - slab * (LINES - 1)) * OWN, OWN), OWN)

    rest = pl.ds(0, (LINES - 1) * OWN)

    @pl.when(is_edge == 0)
    def _():
        one = pl.ds(0, OWN)
        pltpu.make_async_copy(recv2.at[one, :], recv2.at[one, :], recv_sem.at[1]).wait()

    beyond = pltpu.make_async_remote_copy(
        src_ref=recv2.at[edge_tile, :],
        dst_ref=recv2.at[outside, :],
        send_sem=edge_send,
        recv_sem=edge_recv,
        device_id=(me, 1 - slab),
        device_id_type=MESH,
    )
    beyond.start()

    @pl.when(is_edge == 1)
    def _():
        pltpu.make_async_copy(recv2.at[rest, :], recv2.at[rest, :], recv_sem.at[0]).wait()

    @pl.when(is_edge == 0)
    def _():
        less = pl.ds(0, (LINES - 2) * OWN)
        pltpu.make_async_copy(recv2.at[less, :], recv2.at[less, :], recv_sem.at[0]).wait()

    beyond.wait()

    def keep_here(own):
        flags = send1[pl.ds(own, LINES, stride=OWN), :][:, MASK_LANE : MASK_LANE + 1]
        return jnp.where(lane == 0, 1.0, 1.0 - jnp.broadcast_to(flags, (LINES, LANES)))

    fields = []
    for own in range(OWN):
        before, here, after = (recv2[pl.ds(tile * OWN + own, LINES, stride=OWN), :] for tile in range(3))
        fields.append(beside_terms(here, after, before))
    for own, f in enumerate(finish(fields, [functools.partial(keep_here, own) for own in range(OWN)], collide)):
        out_ref[pl.ds(own, MOMENTS, stride=OWN), :] = f.T[:MOMENTS]

    @pl.loop(0, OWN)
    def _(plane):
        near(plane, 0).wait_send()
        near(plane, 1).wait_send()

    pltpu.make_async_copy(send1.at[rest, :], send1.at[rest, :], send_sem.at[0]).wait()
    pltpu.make_async_copy(send2.at[rest, :], send2.at[rest, :], send_sem.at[1]).wait()


def local(moments, mask, coefficients, rates):
    t = tables()
    names = ["to_modes", "forward", "inverse", "series", "cross", "square", "modes_right"]
    constants = [jnp.asarray(t[name]) for name in names]
    in_vmem = pl.BlockSpec(memory_space=pltpu.VMEM)
    in_hbm = pl.BlockSpec(memory_space=pltpu.HBM)
    tile = (NX, LANES)
    line = (OWN, LINES, LANES)
    out = pl.pallas_call(
        kernel,
        out_shape=pltpu.VMEM((MOMENTS * OWN, LINES), F32),
        in_specs=[in_hbm] * (4 + len(constants)),
        out_specs=in_vmem,
        scratch_shapes=[
            pltpu.VMEM((MOMENTS * OWN, LINES), F32),
            pltpu.VMEM((OWN, LINES), jnp.int32),
            pltpu.VMEM((MOMENTS, MOMENTS), F32),
            pltpu.VMEM((1, MOMENTS), F32),
        ]
        + [pltpu.VMEM(c.shape, c.dtype) for c in constants]
        + [pltpu.VMEM(shape, F32) for shape in (
            tile, tile, tile, (NX + 2 * OWN, LANES), (2, *tile), line, (OWN, 2 * HALF, 2 * LANES), (OWN, 2 * HALF, LANES),
            (LANES, LANES), (1, LANES),
        )]
        + [
            pltpu.VMEM((2 * LANES, 2 * LANES), BF16),
            pltpu.VMEM((2 * LANES, 2 * LANES), BF16),
            pltpu.SemaphoreType.DMA((11,)),
            pltpu.SemaphoreType.DMA((2,)),
            pltpu.SemaphoreType.DMA((8,)),
            pltpu.SemaphoreType.DMA((2,)),
            pltpu.SemaphoreType.DMA,
            pltpu.SemaphoreType.DMA,
            pltpu.SemaphoreType.DMA((2, OWN)),
            pltpu.SemaphoreType.DMA((2, OWN)),
        ],
        compiler_params=pltpu.CompilerParams(collective_id=0, has_side_effects=True, vmem_limit_bytes=62 * 1024 * 1024),
        name="duct",
    )(
        moments.reshape(MOMENTS * OWN, LINES),
        mask,
        coefficients,
        rates.reshape(1, MOMENTS),
        *constants,
    )
    return out.reshape(MOMENTS, OWN, LINES)


def solution(mesh):
    in_specs = (P(None, "wa", "gy"), P("wa", "gy"), P(), P())
    return jax.shard_map(local, mesh=mesh, in_specs=in_specs, out_specs=P(None, "wa", "gy"), check_vma=False)
```

```python
import functools
import math

import jax
import jax.numpy as jnp
import ml_dtypes
import numpy as np
from jax import lax
from jax.experimental import pallas as pl
from jax.experimental.pallas import tpu as pltpu
from jax.sharding import PartitionSpec as P

DEG = 7
AXIAL_STEP = 0.2
CROSS_STEP = 0.2
COLLIDE_STEP = 0.5
NX = 1024
LINES = 128
OWN = 8
LANES = 128
DISTANCES = (4, 0, 3, 5, 2, 6, 1, 7)
PLANE = 16
STRIDE = 37
MOMENTS = 120
MASK_LANE = 120
HALF = 72
BLOCKS = HALF // 8
ROOT_HALF = math.sqrt(0.5)

F32 = jnp.float32
BF16 = jnp.bfloat16
MESH = pl.DeviceIdType.MESH


def moment_table():
    entries = []
    for degree in range(DEG + 1):
        for k1 in range(degree, -1, -1):
            for k2 in range(degree - k1, -1, -1):
                entries.append((k1, k2, degree - k1 - k2))
    return entries


def hermite(order, point):
    previous, current = 0.0, 1.0
    for level in range(order):
        previous, current = current, point * current - level * previous
    return current


def hermite_roots(order):
    roots, step = [], 1.0 / 128
    low = -(2.0 * math.sqrt(order) + 1.0) - step / 3
    while len(roots) < order:
        high = low + step
        if (hermite(order, low) > 0) != (hermite(order, high) > 0):
            a, b = low, high
            for _ in range(80):
                middle = 0.5 * (a + b)
                if (hermite(order, middle) > 0) == (hermite(order, a) > 0):
                    a = middle
                else:
                    b = middle
            roots.append(0.5 * (a + b))
        low = high
    return roots


SPEED = hermite_roots(DEG + 1)[-1]


def coupling(entries, lookup, direction):
    matrix = np.zeros((LANES, LANES))
    for position, moment in enumerate(entries):
        raised = list(moment)
        raised[direction] += 1
        partner = lookup.get(tuple(raised))
        if partner is not None:
            matrix[position, partner] = matrix[partner, position] = math.sqrt(raised[direction])
    return matrix


def axial_modes(lookup):
    values = np.zeros(LANES)
    vectors = np.zeros((LANES, LANES))
    column = 0
    for k2 in range(DEG + 1):
        for k3 in range(DEG + 1 - k2):
            size = DEG + 1 - k2 - k3
            for root in hermite_roots(size):
                entry = [hermite(k, root) / math.sqrt(math.factorial(k)) for k in range(size)]
                norm = math.sqrt(sum(v * v for v in entry))
                for k in range(size):
                    vectors[lookup[k, k2, k3], column] = entry[k] / norm
                values[column] = root
                column += 1
    return values, vectors


def parts(table):
    high = table.astype(np.float32).astype(ml_dtypes.bfloat16)
    low = (table - high.astype(np.float64)).astype(np.float32).astype(ml_dtypes.bfloat16)
    return high, low


def right_factor(table):
    high, low = parts(table)
    return np.block([[high, low], [high, low]])


@functools.cache
def tables():
    entries = moment_table()
    lookup = {moment: position for position, moment in enumerate(entries)}
    values, modes = axial_modes(lookup)
    a2 = coupling(entries, lookup, 1)
    eye = np.eye(LANES)

    high, low = parts(modes.T)
    to_modes = np.concatenate([high, high, low], axis=1)

    k1 = np.arange(HALF)
    used = k1 <= 64
    weight = np.where(used, np.where((k1 == 0) | (k1 == 64), 1.0, 2.0), 0.0) / NX
    line = np.arange(LINES)
    forward, inverse = [], []
    for own in range(OWN):
        phase = (((OWN * line + own)[:, None] * k1[None, :]) % NX) * (2 * math.pi / NX)
        cosine, sine = np.cos(phase) * used, np.sin(phase) * used
        forward.append(np.concatenate(parts(np.concatenate([cosine.T, -sine.T], axis=0)), axis=0))
        high, low = parts(np.concatenate([cosine * weight, -sine * weight], axis=1))
        inverse.append(np.concatenate([high, high, low], axis=1))
    forward, inverse = np.stack(forward), np.stack(inverse)

    wave = k1[None, :] + 128 * np.arange(8)[:, None]
    wave = np.where(wave < NX // 2, wave, wave - NX) * (AXIAL_STEP * 2 * math.pi / NX)
    angle = (wave[:, :, None] * values) * used[None, :, None]
    series = np.stack([1 - angle**2 / 2 + angle**4 / 24, -(angle - angle**3 / 6)])
    series = series.astype(np.float32)

    units = [lookup[1, 0, 0], lookup[0, 1, 0], lookup[0, 0, 1]]
    combinations = [(0,), (1,), (2,), (0, 1), (0, 2), (1, 2)]
    spare, target = eye.copy(), np.zeros((LANES, LANES))
    for lane, group in enumerate(combinations, MOMENTS):
        for d in group:
            spare[units[d], lane] = 1.0
    spare[MOMENTS:, MOMENTS:] = 0.0
    for position, moment in enumerate(entries):
        if sum(moment) == 2:
            d = tuple(direction for direction in range(3) for _ in range(moment[direction]))
            if d[0] == d[1]:
                target[MOMENTS + d[0], position] = COLLIDE_STEP * ROOT_HALF
            else:
                target[MOMENTS + combinations.index(d), position] = 0.5 * COLLIDE_STEP
                target[MOMENTS + d[0], position] = target[MOMENTS + d[1], position] = -0.5 * COLLIDE_STEP
    cross = np.concatenate([right_factor(modes.T @ spare), right_factor(modes.T @ (-0.5 * CROSS_STEP * a2) @ spare)])

    degrees = np.array([sum(moment) for moment in entries] + [0] * (LANES - MOMENTS))
    band = (np.abs(degrees[:, None] - degrees[None, :]) <= 1) & (degrees[:, None] >= 2) & (degrees[None, :] >= 2)
    band = (band * COLLIDE_STEP).astype(np.float32)
    target = target.astype(np.float32)
    relaxed = np.diag(COLLIDE_STEP * (degrees >= 2)).astype(np.float32)
    square = np.stack([band, target - relaxed, np.diag(np.arange(LANES) < MOMENTS).astype(np.float32)])
    high, low = parts(modes)
    modes_right = np.concatenate([high, high, low], axis=0)
    return dict(
        to_modes=to_modes, forward=forward, inverse=inverse, series=series, cross=cross, square=square, modes_right=modes_right,
    )


def doubled(a):
    high, low = split(a)
    both = jnp.concatenate([high, low], axis=1)
    return jnp.concatenate([both, both], axis=0)


def split(a):
    high = a.astype(BF16)
    return high, (a - high.astype(F32)).astype(BF16)


def fold(a):
    return a[:, :LANES] + a[:, LANES:]


def add(a, b):
    return (a[0] + b[0], a[1] + b[1])


def sub(a, b):
    return (a[0] - b[0], a[1] - b[1])


def quarter(a, sign):
    return (-a[1], a[0]) if sign > 0 else (a[1], -a[0])


def fourier4(v, sign):
    s, d = add(v[0], v[2]), sub(v[0], v[2])
    t, e = add(v[1], v[3]), quarter(sub(v[1], v[3]), sign)
    return [add(s, t), add(d, e), sub(s, t), sub(d, e)]


def fourier8(v, sign):
    even, odd = fourier4(v[0::2], sign), fourier4(v[1::2], sign)
    turned = [
        odd[0],
        ((odd[1][0] - sign * odd[1][1]) * ROOT_HALF, (odd[1][1] + sign * odd[1][0]) * ROOT_HALF),
        quarter(odd[2], sign),
        ((-odd[3][0] - sign * odd[3][1]) * ROOT_HALF, (-odd[3][1] + sign * odd[3][0]) * ROOT_HALF),
    ]
    return [add(a, b) for a, b in zip(even, turned)] + [sub(a, b) for a, b in zip(even, turned)]


def device_at(place):
    chip, core = place // 2, place % 2
    x_hi = chip // 32
    turn = chip % 32
    turn = turn + x_hi * (31 - 2 * turn)
    z = turn // 4
    y = turn % 4
    y = y + (z % 2) * (3 - 2 * y)
    return ((z * 2 + x_hi) * 4 + y) * 2 + core


def place_of(device):
    core, y, x_hi, z = device & 1, (device >> 1) & 3, (device >> 3) & 1, device >> 4
    turn = z * 4 + y + (z & 1) * (3 - 2 * y)
    return (x_hi * 32 + turn + x_hi * (31 - 2 * turn)) * 2 + core


def kernel(
    x_h, mask_h, c_h, rate_h,
    to_modes_h, forward_h, inverse_h, series_h, cross_h, square_h, modes_h,
    out_ref,
    x_ref, mask_ref, c_ref, rate_ref, to_modes, forward, inverse, series, cross, square, modes,
    send1, recv1, send2, recv2, beside, wall, pair, spectrum, padded, rate_row, collide, advance_modes,
    table_sem, send_sem, plane_recv, recv_sem, edge_send, edge_recv, near_send, near_recv,
):
    me, slab = lax.axis_index("wa"), lax.axis_index("gy")
    place = place_of(me)
    my_line = place + slab * (LINES - 1 - 2 * place)
    is_edge = place // (LINES - 1)
    next_wa, next_gy = device_at(place + 1 - is_edge), slab + is_edge * (1 - 2 * slab)
    is_first = 1 - (place + LINES - 1) // LINES
    prev_wa, prev_gy = device_at(place - 1 + is_first), slab + is_first * (1 - 2 * slab)

    loads = [
        pltpu.make_async_copy(src, dst, table_sem.at[i])
        for i, (src, dst) in enumerate(
            [(x_h, x_ref), (mask_h, mask_ref), (to_modes_h, to_modes), (c_h, c_ref), (rate_h, rate_ref), (forward_h, forward),
             (series_h, series), (inverse_h, inverse), (cross_h, cross), (square_h, square), (modes_h, modes)]
        )
    ]
    for load in loads[:3]:
        load.start()

    barrier = pltpu.get_barrier_semaphore()

    @pl.loop(1, LINES, unroll=8)
    def _(step):
        pl.semaphore_signal(barrier, inc=1, device_id=((me + step) & (LINES - 1), slab), device_id_type=MESH)

    pl.semaphore_signal(barrier, inc=1, device_id=(me, 1 - slab), device_id_type=MESH)

    for load in loads[3:]:
        load.start()
    for load in loads[:3]:
        load.wait()

    row = lax.broadcasted_iota(jnp.int32, (LANES, LANES), 0)
    lane = lax.broadcasted_iota(jnp.int32, (LANES, LANES), 1)

    turned = []
    for own in range(OWN):
        cells = x_ref[pl.ds(own, MOMENTS, stride=OWN), :]
        cells = jnp.concatenate([cells, jnp.zeros((LANES - MOMENTS, LANES), F32)], axis=0)
        high, low = split(cells)
        turned.append(jnp.dot(to_modes[...], jnp.concatenate([high, low, high], axis=0), preferred_element_type=F32))
    for own in range(OWN):
        flags = mask_ref[pl.ds(own, 1), :].astype(F32)
        send1[pl.ds(own, LINES, stride=OWN), :] = jnp.where(row == MASK_LANE, flags, turned[own]).T

    pl.semaphore_wait(barrier, LINES)

    z = me >> 4

    def serve1(target):
        target_place = place_of(target)
        target_line = target_place + slab * (LINES - 1 - 2 * target_place)
        pltpu.make_async_remote_copy(
            src_ref=send1.at[pl.ds(pl.multiple_of(target_line * OWN, OWN), OWN), :],
            dst_ref=recv1.at[pl.ds(pl.multiple_of(me * OWN, OWN), OWN), :],
            send_sem=send_sem.at[0],
            recv_sem=plane_recv.at[z],
            device_id=(target, slab),
            device_id_type=MESH,
        ).start()

    for first in range(0, 8, 2):
        pair_of = DISTANCES[first : first + 2]

        @pl.loop(0, PLANE)
        def _(step):
            for distance in pair_of:
                if distance:
                    serve1(((z + distance) & 7) * PLANE + ((me + step) & (PLANE - 1)))

        if 0 in pair_of:

            @pl.loop(1, PLANE)
            def _(step):
                serve1(z * PLANE + ((me + step) & (PLANE - 1)))

    recv1[pl.ds(pl.multiple_of(me * OWN, OWN), OWN), :] = send1[pl.ds(pl.multiple_of(my_line * OWN, OWN), OWN), :]

    for load in loads[3:]:
        load.wait()
    padded[...] = jnp.zeros_like(padded)
    padded[:MOMENTS, :MOMENTS] = c_ref[...]
    rate_row[...] = jnp.zeros_like(rate_row)
    rate_row[:, :MOMENTS] = rate_ref[...]
    linear = (padded[...] * square[0]).T + square[1] * rate_row[...] + square[2]
    collide[...] = doubled(linear)
    high, low = split(linear)
    linear = jnp.dot(jnp.concatenate([high, low, high], axis=1), modes[...], preferred_element_type=F32)
    advance_modes[...] = doubled(linear)

    def beside_terms(here, after, before):
        return here * (1 - CROSS_STEP * SPEED) + (after + before) * (0.5 * CROSS_STEP * SPEED), after - before

    def finish(fields, keeps, factor):
        moved = []
        for (here, differences), keep in zip(fields, keeps):
            operand = jnp.concatenate([*split(here), *split(differences)], axis=1)
            moved.append(fold(jnp.dot(operand, cross[...], preferred_element_type=F32)) * keep())
        moved = [jnp.where(lane >= MOMENTS, f * f, f) for f in moved]
        return [fold(jnp.dot(jnp.concatenate(split(f), axis=1), factor[...], preferred_element_type=F32)) for f in moved]

    def to_spectrum(own, cells):
        table = forward[own]
        both = jnp.dot(jnp.concatenate([table, table], axis=1), jnp.concatenate(split(cells), axis=0), preferred_element_type=F32)
        return both[: 2 * HALF] + both[2 * HALF :]

    def advance(spectrum, start):
        lanes = pl.ds(start, LANES)

        @pl.loop(0, BLOCKS, unroll=3)
        def _(block):
            at = pl.multiple_of(block * 8, 8)
            re, im = pl.ds(at, 8), pl.ds(pl.multiple_of(HALF + at, 8), 8)
            f = fourier8([(spectrum[own, re, lanes], spectrum[own, im, lanes]) for own in range(OWN)], -1)
            h = []
            for k, (fr, fi) in enumerate(f):
                pr, pi = series[0, k, re, :], series[1, k, re, :]
                h.append((pr * fr - pi * fi, pr * fi + pi * fr))
            for own, (ur, ui) in enumerate(fourier8(h, 1)):
                spectrum[own, re, lanes] = ur
                spectrum[own, im, lanes] = ui

    def from_spectrum(own, values):
        high, low = split(values)
        return jnp.dot(inverse[own], jnp.concatenate([high, low, high], axis=0), preferred_element_type=F32)

    def near(plane, which):
        slot = 1 - is_first if which else is_edge
        part = pl.ds(pl.multiple_of(plane * (PLANE * OWN), PLANE * OWN), PLANE * OWN)
        return pltpu.make_async_remote_copy(
            src_ref=recv1.at[part, :],
            dst_ref=beside.at[slot, part, :],
            send_sem=near_send.at[which, plane],
            recv_sem=near_recv.at[slot, plane],
            device_id=(prev_wa, prev_gy) if which else (next_wa, next_gy),
            device_id_type=MESH,
        )

    for distance in DISTANCES:
        plane = (z - distance) & 7
        part = pl.ds(0, (PLANE if distance else PLANE - 1) * OWN)
        pltpu.make_async_copy(recv1.at[part, :], recv1.at[part, :], plane_recv.at[plane]).wait()
        near(plane, 0).start()
        near(plane, 1).start()

    for own in range(OWN):
        flags = recv1[pl.ds(own, LINES, stride=OWN), :][:, MASK_LANE : MASK_LANE + 1]
        wall[own] = jnp.where(lane == 0, 1.0, 1.0 - jnp.broadcast_to(flags, (LINES, LANES)))

    @pl.loop(0, OWN)
    def _(plane):
        part = pl.ds(pl.multiple_of(plane * (PLANE * OWN), PLANE * OWN), PLANE * OWN)
        for slot in range(2):
            pltpu.make_async_copy(recv1.at[part, :], beside.at[slot, part, :], near_recv.at[slot, plane]).wait()

    inside = 1.0 - is_first.astype(F32)
    upward = 1.0 - 2.0 * slab.astype(F32)

    fields = []
    for own in range(OWN):
        rows = pl.ds(own, LINES, stride=OWN)
        cells = recv1[rows, :]
        here, differences = beside_terms(cells, beside[1, rows, :], beside[0, rows, :] * inside)
        fields.append(jnp.concatenate([here, differences * upward], axis=1))
    for own, field in enumerate(fields):
        pair[own] = to_spectrum(own, field)

    advance(pair, 0)
    advance(pair, LANES)

    fields = [from_spectrum(own, pair[own]) for own in range(OWN)]
    fields = [(f[:, :LANES], f[:, LANES:]) for f in fields]
    for own, f in enumerate(finish(fields, [functools.partial(wall.__getitem__, own) for own in range(OWN)], advance_modes)):
        spectrum[own] = to_spectrum(own, f)

    advance(spectrum, 0)

    for own, lines in enumerate([from_spectrum(own, spectrum[own]) for own in range(OWN)]):
        send2[pl.ds(own, LINES, stride=OWN), :] = lines

    my_tile = pl.ds(pl.multiple_of((my_line + 1) * OWN, OWN), OWN)

    @pl.loop(1, LINES)
    def _(step):
        target = (me + ((step + 1) >> 1) * (STRIDE * (2 * (step & 1) - 1))) & (LINES - 1)
        pltpu.make_async_remote_copy(
            src_ref=send2.at[pl.ds(pl.multiple_of(target * OWN, OWN), OWN), :],
            dst_ref=recv2.at[my_tile, :],
            send_sem=send_sem.at[1],
            recv_sem=recv_sem.at[is_edge],
            device_id=(target, slab),
            device_id_type=MESH,
        ).start()

    recv2[my_tile, :] = send2[pl.ds(pl.multiple_of(me * OWN, OWN), OWN), :]
    outside = pl.ds(pl.multiple_of(slab * (LINES + 1) * OWN, OWN), OWN)
    recv2[outside, :] = jnp.zeros((OWN, LANES), F32)

    edge_tile = pl.ds(pl.multiple_of((LINES - slab * (LINES - 1)) * OWN, OWN), OWN)

    rest = pl.ds(0, (LINES - 1) * OWN)

    @pl.when(is_edge == 0)
    def _():
        one = pl.ds(0, OWN)
        pltpu.make_async_copy(recv2.at[one, :], recv2.at[one, :], recv_sem.at[1]).wait()

    beyond = pltpu.make_async_remote_copy(
        src_ref=recv2.at[edge_tile, :],
        dst_ref=recv2.at[outside, :],
        send_sem=edge_send,
        recv_sem=edge_recv,
        device_id=(me, 1 - slab),
        device_id_type=MESH,
    )
    beyond.start()

    @pl.when(is_edge == 1)
    def _():
        pltpu.make_async_copy(recv2.at[rest, :], recv2.at[rest, :], recv_sem.at[0]).wait()

    @pl.when(is_edge == 0)
    def _():
        less = pl.ds(0, (LINES - 2) * OWN)
        pltpu.make_async_copy(recv2.at[less, :], recv2.at[less, :], recv_sem.at[0]).wait()

    beyond.wait()

    def keep_here(own):
        flags = send1[pl.ds(own, LINES, stride=OWN), :][:, MASK_LANE : MASK_LANE + 1]
        return jnp.where(lane == 0, 1.0, 1.0 - jnp.broadcast_to(flags, (LINES, LANES)))

    fields = []
    for own in range(OWN):
        before, here, after = (recv2[pl.ds(tile * OWN + own, LINES, stride=OWN), :] for tile in range(3))
        fields.append(beside_terms(here, after, before))
    for own, f in enumerate(finish(fields, [functools.partial(keep_here, own) for own in range(OWN)], collide)):
        out_ref[pl.ds(own, MOMENTS, stride=OWN), :] = f.T[:MOMENTS]

    @pl.loop(0, OWN)
    def _(plane):
        near(plane, 0).wait_send()
        near(plane, 1).wait_send()

    pltpu.make_async_copy(send1.at[rest, :], send1.at[rest, :], send_sem.at[0]).wait()
    pltpu.make_async_copy(send2.at[rest, :], send2.at[rest, :], send_sem.at[1]).wait()


def local(moments, mask, coefficients, rates):
    t = tables()
    names = ["to_modes", "forward", "inverse", "series", "cross", "square", "modes_right"]
    constants = [jnp.asarray(t[name]) for name in names]
    in_vmem = pl.BlockSpec(memory_space=pltpu.VMEM)
    in_hbm = pl.BlockSpec(memory_space=pltpu.HBM)
    tile = (NX, LANES)
    line = (OWN, LINES, LANES)
    out = pl.pallas_call(
        kernel,
        out_shape=pltpu.VMEM((MOMENTS * OWN, LINES), F32),
        in_specs=[in_hbm] * (4 + len(constants)),
        out_specs=in_vmem,
        scratch_shapes=[
            pltpu.VMEM((MOMENTS * OWN, LINES), F32),
            pltpu.VMEM((OWN, LINES), jnp.int32),
            pltpu.VMEM((MOMENTS, MOMENTS), F32),
            pltpu.VMEM((1, MOMENTS), F32),
        ]
        + [pltpu.VMEM(c.shape, c.dtype) for c in constants]
        + [pltpu.VMEM(shape, F32) for shape in (
            tile, tile, tile, (NX + 2 * OWN, LANES), (2, *tile), line, (OWN, 2 * HALF, 2 * LANES), (OWN, 2 * HALF, LANES),
            (LANES, LANES), (1, LANES),
        )]
        + [
            pltpu.VMEM((2 * LANES, 2 * LANES), BF16),
            pltpu.VMEM((2 * LANES, 2 * LANES), BF16),
            pltpu.SemaphoreType.DMA((11,)),
            pltpu.SemaphoreType.DMA((2,)),
            pltpu.SemaphoreType.DMA((8,)),
            pltpu.SemaphoreType.DMA((2,)),
            pltpu.SemaphoreType.DMA,
            pltpu.SemaphoreType.DMA,
            pltpu.SemaphoreType.DMA((2, OWN)),
            pltpu.SemaphoreType.DMA((2, OWN)),
        ],
        compiler_params=pltpu.CompilerParams(collective_id=0, has_side_effects=True, vmem_limit_bytes=62 * 1024 * 1024),
        name="duct",
    )(
        moments.reshape(MOMENTS * OWN, LINES),
        mask,
        coefficients,
        rates.reshape(1, MOMENTS),
        *constants,
    )
    return out.reshape(MOMENTS, OWN, LINES)


def solution(mesh):
    in_specs = (P(None, "wa", "gy"), P("wa", "gy"), P(), P())
    return jax.shard_map(local, mesh=mesh, in_specs=in_specs, out_specs=P(None, "wa", "gy"), check_vma=False)
```

```python
import functools
import math

import jax
import jax.numpy as jnp
import ml_dtypes
import numpy as np
from jax import lax
from jax.experimental import pallas as pl
from jax.experimental.pallas import tpu as pltpu
from jax.sharding import PartitionSpec as P

DEG = 7
AXIAL_STEP = 0.2
CROSS_STEP = 0.2
COLLIDE_STEP = 0.5
NX = 1024
LINES = 128
OWN = 8
LANES = 128
DISTANCES = (4, 0, 3, 5, 2, 6, 1, 7)
PLANE = 16
STRIDE = 37
MOMENTS = 120
MASK_LANE = 120
HALF = 72
BLOCKS = HALF // 8
ROOT_HALF = math.sqrt(0.5)

F32 = jnp.float32
BF16 = jnp.bfloat16
MESH = pl.DeviceIdType.MESH


def moment_table():
    entries = []
    for degree in range(DEG + 1):
        for k1 in range(degree, -1, -1):
            for k2 in range(degree - k1, -1, -1):
                entries.append((k1, k2, degree - k1 - k2))
    return entries


def hermite(order, point):
    previous, current = 0.0, 1.0
    for level in range(order):
        previous, current = current, point * current - level * previous
    return current


def hermite_roots(order):
    roots, step = [], 1.0 / 128
    low = -(2.0 * math.sqrt(order) + 1.0) - step / 3
    while len(roots) < order:
        high = low + step
        if (hermite(order, low) > 0) != (hermite(order, high) > 0):
            a, b = low, high
            for _ in range(80):
                middle = 0.5 * (a + b)
                if (hermite(order, middle) > 0) == (hermite(order, a) > 0):
                    a = middle
                else:
                    b = middle
            roots.append(0.5 * (a + b))
        low = high
    return roots


SPEED = hermite_roots(DEG + 1)[-1]


def coupling(entries, lookup, direction):
    matrix = np.zeros((LANES, LANES))
    for position, moment in enumerate(entries):
        raised = list(moment)
        raised[direction] += 1
        partner = lookup.get(tuple(raised))
        if partner is not None:
            matrix[position, partner] = matrix[partner, position] = math.sqrt(raised[direction])
    return matrix


def axial_modes(lookup):
    values = np.zeros(LANES)
    vectors = np.zeros((LANES, LANES))
    column = 0
    for k2 in range(DEG + 1):
        for k3 in range(DEG + 1 - k2):
            size = DEG + 1 - k2 - k3
            for root in hermite_roots(size):
                entry = [hermite(k, root) / math.sqrt(math.factorial(k)) for k in range(size)]
                norm = math.sqrt(sum(v * v for v in entry))
                for k in range(size):
                    vectors[lookup[k, k2, k3], column] = entry[k] / norm
                values[column] = root
                column += 1
    return values, vectors


def parts(table):
    high = table.astype(np.float32).astype(ml_dtypes.bfloat16)
    low = (table - high.astype(np.float64)).astype(np.float32).astype(ml_dtypes.bfloat16)
    return high, low


def right_factor(table):
    high, low = parts(table)
    return np.block([[high, low], [high, low]])


@functools.cache
def tables():
    entries = moment_table()
    lookup = {moment: position for position, moment in enumerate(entries)}
    values, modes = axial_modes(lookup)
    a2 = coupling(entries, lookup, 1)
    eye = np.eye(LANES)

    high, low = parts(modes.T)
    to_modes = np.concatenate([high, high, low], axis=1)

    k1 = np.arange(HALF)
    used = k1 <= 64
    weight = np.where(used, np.where((k1 == 0) | (k1 == 64), 1.0, 2.0), 0.0) / NX
    line = np.arange(LINES)
    forward, inverse = [], []
    for own in range(OWN):
        phase = (((OWN * line + own)[:, None] * k1[None, :]) % NX) * (2 * math.pi / NX)
        cosine, sine = np.cos(phase) * used, np.sin(phase) * used
        forward.append(np.concatenate(parts(np.concatenate([cosine.T, -sine.T], axis=0)), axis=0))
        high, low = parts(np.concatenate([cosine * weight, -sine * weight], axis=1))
        inverse.append(np.concatenate([high, high, low], axis=1))
    forward, inverse = np.stack(forward), np.stack(inverse)

    wave = k1[None, :] + 128 * np.arange(8)[:, None]
    wave = np.where(wave < NX // 2, wave, wave - NX) * (AXIAL_STEP * 2 * math.pi / NX)
    angle = (wave[:, :, None] * values) * used[None, :, None]
    series = np.stack([1 - angle**2 / 2 + angle**4 / 24, -(angle - angle**3 / 6)])
    series = series.astype(np.float32)

    units = [lookup[1, 0, 0], lookup[0, 1, 0], lookup[0, 0, 1]]
    combinations = [(0,), (1,), (2,), (0, 1), (0, 2), (1, 2)]
    spare, target = eye.copy(), np.zeros((LANES, LANES))
    for lane, group in enumerate(combinations, MOMENTS):
        for d in group:
            spare[units[d], lane] = 1.0
    spare[MOMENTS:, MOMENTS:] = 0.0
    for position, moment in enumerate(entries):
        if sum(moment) == 2:
            d = tuple(direction for direction in range(3) for _ in range(moment[direction]))
            if d[0] == d[1]:
                target[MOMENTS + d[0], position] = COLLIDE_STEP * ROOT_HALF
            else:
                target[MOMENTS + combinations.index(d), position] = 0.5 * COLLIDE_STEP
                target[MOMENTS + d[0], position] = target[MOMENTS + d[1], position] = -0.5 * COLLIDE_STEP
    cross = np.concatenate([right_factor(modes.T @ spare), right_factor(modes.T @ (-0.5 * CROSS_STEP * a2) @ spare)])

    degrees = np.array([sum(moment) for moment in entries] + [0] * (LANES - MOMENTS))
    band = (np.abs(degrees[:, None] - degrees[None, :]) <= 1) & (degrees[:, None] >= 2) & (degrees[None, :] >= 2)
    band = (band * COLLIDE_STEP).astype(np.float32)
    target = target.astype(np.float32)
    relaxed = np.diag(COLLIDE_STEP * (degrees >= 2)).astype(np.float32)
    square = np.stack([band, target - relaxed, np.diag(np.arange(LANES) < MOMENTS).astype(np.float32)])
    high, low = parts(modes)
    modes_right = np.concatenate([high, high, low], axis=0)
    return dict(
        to_modes=to_modes, forward=forward, inverse=inverse, series=series, cross=cross, square=square, modes_right=modes_right,
    )


def doubled(a):
    high, low = split(a)
    both = jnp.concatenate([high, low], axis=1)
    return jnp.concatenate([both, both], axis=0)


def split(a):
    high = a.astype(BF16)
    return high, (a - high.astype(F32)).astype(BF16)


def fold(a):
    return a[:, :LANES] + a[:, LANES:]


def add(a, b):
    return (a[0] + b[0], a[1] + b[1])


def sub(a, b):
    return (a[0] - b[0], a[1] - b[1])


def quarter(a, sign):
    return (-a[1], a[0]) if sign > 0 else (a[1], -a[0])


def fourier4(v, sign):
    s, d = add(v[0], v[2]), sub(v[0], v[2])
    t, e = add(v[1], v[3]), quarter(sub(v[1], v[3]), sign)
    return [add(s, t), add(d, e), sub(s, t), sub(d, e)]


def fourier8(v, sign):
    even, odd = fourier4(v[0::2], sign), fourier4(v[1::2], sign)
    turned = [
        odd[0],
        ((odd[1][0] - sign * odd[1][1]) * ROOT_HALF, (odd[1][1] + sign * odd[1][0]) * ROOT_HALF),
        quarter(odd[2], sign),
        ((-odd[3][0] - sign * odd[3][1]) * ROOT_HALF, (-odd[3][1] + sign * odd[3][0]) * ROOT_HALF),
    ]
    return [add(a, b) for a, b in zip(even, turned)] + [sub(a, b) for a, b in zip(even, turned)]


def device_at(place):
    chip, core = place // 2, place % 2
    x_hi = chip // 32
    turn = chip % 32
    turn = turn + x_hi * (31 - 2 * turn)
    z = turn // 4
    y = turn % 4
    y = y + (z % 2) * (3 - 2 * y)
    return ((z * 2 + x_hi) * 4 + y) * 2 + core


def place_of(device):
    core, y, x_hi, z = device & 1, (device >> 1) & 3, (device >> 3) & 1, device >> 4
    turn = z * 4 + y + (z & 1) * (3 - 2 * y)
    return (x_hi * 32 + turn + x_hi * (31 - 2 * turn)) * 2 + core


def kernel(
    x_h, mask_h, c_h, rate_h,
    to_modes_h, forward_h, inverse_h, series_h, cross_h, square_h, modes_h,
    out_ref,
    x_ref, mask_ref, c_ref, rate_ref, to_modes, forward, inverse, series, cross, square, modes,
    send1, recv1, send2, recv2, beside, wall, pair, spectrum, padded, rate_row, collide, advance_modes,
    table_sem, send_sem, plane_recv, recv_sem, edge_send, edge_recv, near_send, near_recv,
):
    me, slab = lax.axis_index("wa"), lax.axis_index("gy")
    place = place_of(me)
    my_line = place + slab * (LINES - 1 - 2 * place)
    is_edge = place // (LINES - 1)
    next_wa, next_gy = device_at(place + 1 - is_edge), slab + is_edge * (1 - 2 * slab)
    is_first = 1 - (place + LINES - 1) // LINES
    prev_wa, prev_gy = device_at(place - 1 + is_first), slab + is_first * (1 - 2 * slab)

    loads = [
        pltpu.make_async_copy(src, dst, table_sem.at[i])
        for i, (src, dst) in enumerate(
            [(x_h, x_ref), (mask_h, mask_ref), (to_modes_h, to_modes), (c_h, c_ref), (rate_h, rate_ref), (forward_h, forward),
             (series_h, series), (inverse_h, inverse), (cross_h, cross), (square_h, square), (modes_h, modes)]
        )
    ]
    for load in loads[:3]:
        load.start()

    barrier = pltpu.get_barrier_semaphore()

    @pl.loop(1, LINES, unroll=8)
    def _(step):
        pl.semaphore_signal(barrier, inc=1, device_id=((me + step) & (LINES - 1), slab), device_id_type=MESH)

    pl.semaphore_signal(barrier, inc=1, device_id=(me, 1 - slab), device_id_type=MESH)

    for load in loads[3:]:
        load.start()
    for load in loads[:3]:
        load.wait()

    row = lax.broadcasted_iota(jnp.int32, (LANES, LANES), 0)
    lane = lax.broadcasted_iota(jnp.int32, (LANES, LANES), 1)

    turned = []
    for own in range(OWN):
        cells = x_ref[pl.ds(own, MOMENTS, stride=OWN), :]
        cells = jnp.concatenate([cells, jnp.zeros((LANES - MOMENTS, LANES), F32)], axis=0)
        high, low = split(cells)
        turned.append(jnp.dot(to_modes[...], jnp.concatenate([high, low, high], axis=0), preferred_element_type=F32))
    for own in range(OWN):
        flags = mask_ref[pl.ds(own, 1), :].astype(F32)
        send1[pl.ds(own, LINES, stride=OWN), :] = jnp.where(row == MASK_LANE, flags, turned[own]).T

    pl.semaphore_wait(barrier, LINES)

    z = me >> 4

    def serve1(target):
        target_place = place_of(target)
        target_line = target_place + slab * (LINES - 1 - 2 * target_place)
        pltpu.make_async_remote_copy(
            src_ref=send1.at[pl.ds(pl.multiple_of(target_line * OWN, OWN), OWN), :],
            dst_ref=recv1.at[pl.ds(pl.multiple_of(me * OWN, OWN), OWN), :],
            send_sem=send_sem.at[0],
            recv_sem=plane_recv.at[z],
            device_id=(target, slab),
            device_id_type=MESH,
        ).start()

    for first in range(0, 8, 2):
        pair_of = DISTANCES[first : first + 2]

        @pl.loop(0, PLANE)
        def _(step):
            for distance in pair_of:
                if distance:
                    serve1(((z + distance) & 7) * PLANE + ((me + step) & (PLANE - 1)))

        if 0 in pair_of:

            @pl.loop(1, PLANE)
            def _(step):
                serve1(z * PLANE + ((me + step) & (PLANE - 1)))

    recv1[pl.ds(pl.multiple_of(me * OWN, OWN), OWN), :] = send1[pl.ds(pl.multiple_of(my_line * OWN, OWN), OWN), :]

    for load in loads[3:]:
        load.wait()
    padded[...] = jnp.zeros_like(padded)
    padded[:MOMENTS, :MOMENTS] = c_ref[...]
    rate_row[...] = jnp.zeros_like(rate_row)
    rate_row[:, :MOMENTS] = rate_ref[...]
    linear = (padded[...] * square[0]).T + square[1] * rate_row[...] + square[2]
    collide[...] = doubled(linear)
    high, low = split(linear)
    linear = jnp.dot(jnp.concatenate([high, low, high], axis=1), modes[...], preferred_element_type=F32)
    advance_modes[...] = doubled(linear)

    def beside_terms(here, after, before):
        return here * (1 - CROSS_STEP * SPEED) + (after + before) * (0.5 * CROSS_STEP * SPEED), after - before

    def finish(fields, keeps, factor):
        moved = []
        for (here, differences), keep in zip(fields, keeps):
            operand = jnp.concatenate([*split(here), *split(differences)], axis=1)
            moved.append(fold(jnp.dot(operand, cross[...], preferred_element_type=F32)) * keep())
        moved = [jnp.where(lane >= MOMENTS, f * f, f) for f in moved]
        return [fold(jnp.dot(jnp.concatenate(split(f), axis=1), factor[...], preferred_element_type=F32)) for f in moved]

    def to_spectrum(own, cells):
        table = forward[own]
        both = jnp.dot(jnp.concatenate([table, table], axis=1), jnp.concatenate(split(cells), axis=0), preferred_element_type=F32)
        return both[: 2 * HALF] + both[2 * HALF :]

    def advance(spectrum, start):
        lanes = pl.ds(start, LANES)

        @pl.loop(0, BLOCKS, unroll=True)
        def _(block):
            at = pl.multiple_of(block * 8, 8)
            re, im = pl.ds(at, 8), pl.ds(pl.multiple_of(HALF + at, 8), 8)
            f = fourier8([(spectrum[own, re, lanes], spectrum[own, im, lanes]) for own in range(OWN)], -1)
            h = []
            for k, (fr, fi) in enumerate(f):
                pr, pi = series[0, k, re, :], series[1, k, re, :]
                h.append((pr * fr - pi * fi, pr * fi + pi * fr))
            for own, (ur, ui) in enumerate(fourier8(h, 1)):
                spectrum[own, re, lanes] = ur
                spectrum[own, im, lanes] = ui

    def from_spectrum(own, values):
        high, low = split(values)
        return jnp.dot(inverse[own], jnp.concatenate([high, low, high], axis=0), preferred_element_type=F32)

    def near(plane, which):
        slot = 1 - is_first if which else is_edge
        part = pl.ds(pl.multiple_of(plane * (PLANE * OWN), PLANE * OWN), PLANE * OWN)
        return pltpu.make_async_remote_copy(
            src_ref=recv1.at[part, :],
            dst_ref=beside.at[slot, part, :],
            send_sem=near_send.at[which, plane],
            recv_sem=near_recv.at[slot, plane],
            device_id=(prev_wa, prev_gy) if which else (next_wa, next_gy),
            device_id_type=MESH,
        )

    for distance in DISTANCES:
        plane = (z - distance) & 7
        part = pl.ds(0, (PLANE if distance else PLANE - 1) * OWN)
        pltpu.make_async_copy(recv1.at[part, :], recv1.at[part, :], plane_recv.at[plane]).wait()
        near(plane, 0).start()
        near(plane, 1).start()

    for own in range(OWN):
        flags = recv1[pl.ds(own, LINES, stride=OWN), :][:, MASK_LANE : MASK_LANE + 1]
        wall[own] = jnp.where(lane == 0, 1.0, 1.0 - jnp.broadcast_to(flags, (LINES, LANES)))

    @pl.loop(0, OWN)
    def _(plane):
        part = pl.ds(pl.multiple_of(plane * (PLANE * OWN), PLANE * OWN), PLANE * OWN)
        for slot in range(2):
            pltpu.make_async_copy(recv1.at[part, :], beside.at[slot, part, :], near_recv.at[slot, plane]).wait()

    inside = 1.0 - is_first.astype(F32)
    upward = 1.0 - 2.0 * slab.astype(F32)

    fields = []
    for own in range(OWN):
        rows = pl.ds(own, LINES, stride=OWN)
        cells = recv1[rows, :]
        here, differences = beside_terms(cells, beside[1, rows, :], beside[0, rows, :] * inside)
        fields.append(jnp.concatenate([here, differences * upward], axis=1))
    for own, field in enumerate(fields):
        pair[own] = to_spectrum(own, field)

    advance(pair, 0)
    advance(pair, LANES)

    fields = [from_spectrum(own, pair[own]) for own in range(OWN)]
    fields = [(f[:, :LANES], f[:, LANES:]) for f in fields]
    for own, f in enumerate(finish(fields, [functools.partial(wall.__getitem__, own) for own in range(OWN)], advance_modes)):
        spectrum[own] = to_spectrum(own, f)

    advance(spectrum, 0)

    for own, lines in enumerate([from_spectrum(own, spectrum[own]) for own in range(OWN)]):
        send2[pl.ds(own, LINES, stride=OWN), :] = lines

    my_tile = pl.ds(pl.multiple_of((my_line + 1) * OWN, OWN), OWN)

    @pl.loop(1, LINES)
    def _(step):
        target = (me + ((step + 1) >> 1) * (STRIDE * (2 * (step & 1) - 1))) & (LINES - 1)
        pltpu.make_async_remote_copy(
            src_ref=send2.at[pl.ds(pl.multiple_of(target * OWN, OWN), OWN), :],
            dst_ref=recv2.at[my_tile, :],
            send_sem=send_sem.at[1],
            recv_sem=recv_sem.at[is_edge],
            device_id=(target, slab),
            device_id_type=MESH,
        ).start()

    for own in range(OWN):
        flags = send1[pl.ds(own, LINES, stride=OWN), :][:, MASK_LANE : MASK_LANE + 1]
        wall[own] = jnp.where(lane == 0, 1.0, 1.0 - jnp.broadcast_to(flags, (LINES, LANES)))

    recv2[my_tile, :] = send2[pl.ds(pl.multiple_of(me * OWN, OWN), OWN), :]
    outside = pl.ds(pl.multiple_of(slab * (LINES + 1) * OWN, OWN), OWN)
    recv2[outside, :] = jnp.zeros((OWN, LANES), F32)

    edge_tile = pl.ds(pl.multiple_of((LINES - slab * (LINES - 1)) * OWN, OWN), OWN)

    rest = pl.ds(0, (LINES - 1) * OWN)

    @pl.when(is_edge == 0)
    def _():
        one = pl.ds(0, OWN)
        pltpu.make_async_copy(recv2.at[one, :], recv2.at[one, :], recv_sem.at[1]).wait()

    beyond = pltpu.make_async_remote_copy(
        src_ref=recv2.at[edge_tile, :],
        dst_ref=recv2.at[outside, :],
        send_sem=edge_send,
        recv_sem=edge_recv,
        device_id=(me, 1 - slab),
        device_id_type=MESH,
    )
    beyond.start()

    @pl.when(is_edge == 1)
    def _():
        pltpu.make_async_copy(recv2.at[rest, :], recv2.at[rest, :], recv_sem.at[0]).wait()

    @pl.when(is_edge == 0)
    def _():
        less = pl.ds(0, (LINES - 2) * OWN)
        pltpu.make_async_copy(recv2.at[less, :], recv2.at[less, :], recv_sem.at[0]).wait()

    beyond.wait()

    fields = []
    for own in range(OWN):
        before, here, after = (recv2[pl.ds(tile * OWN + own, LINES, stride=OWN), :] for tile in range(3))
        fields.append(beside_terms(here, after, before))
    for own, f in enumerate(finish(fields, [functools.partial(wall.__getitem__, own) for own in range(OWN)], collide)):
        out_ref[pl.ds(own, MOMENTS, stride=OWN), :] = f.T[:MOMENTS]

    @pl.loop(0, OWN)
    def _(plane):
        near(plane, 0).wait_send()
        near(plane, 1).wait_send()

    pltpu.make_async_copy(send1.at[rest, :], send1.at[rest, :], send_sem.at[0]).wait()
    pltpu.make_async_copy(send2.at[rest, :], send2.at[rest, :], send_sem.at[1]).wait()


def local(moments, mask, coefficients, rates):
    t = tables()
    names = ["to_modes", "forward", "inverse", "series", "cross", "square", "modes_right"]
    constants = [jnp.asarray(t[name]) for name in names]
    in_vmem = pl.BlockSpec(memory_space=pltpu.VMEM)
    in_hbm = pl.BlockSpec(memory_space=pltpu.HBM)
    tile = (NX, LANES)
    line = (OWN, LINES, LANES)
    out = pl.pallas_call(
        kernel,
        out_shape=pltpu.VMEM((MOMENTS * OWN, LINES), F32),
        in_specs=[in_hbm] * (4 + len(constants)),
        out_specs=in_vmem,
        scratch_shapes=[
            pltpu.VMEM((MOMENTS * OWN, LINES), F32),
            pltpu.VMEM((OWN, LINES), jnp.int32),
            pltpu.VMEM((MOMENTS, MOMENTS), F32),
            pltpu.VMEM((1, MOMENTS), F32),
        ]
        + [pltpu.VMEM(c.shape, c.dtype) for c in constants]
        + [pltpu.VMEM(shape, F32) for shape in (
            tile, tile, tile, (NX + 2 * OWN, LANES), (2, *tile), line, (OWN, 2 * HALF, 2 * LANES), (OWN, 2 * HALF, LANES),
            (LANES, LANES), (1, LANES),
        )]
        + [
            pltpu.VMEM((2 * LANES, 2 * LANES), BF16),
            pltpu.VMEM((2 * LANES, 2 * LANES), BF16),
            pltpu.SemaphoreType.DMA((11,)),
            pltpu.SemaphoreType.DMA((2,)),
            pltpu.SemaphoreType.DMA((8,)),
            pltpu.SemaphoreType.DMA((2,)),
            pltpu.SemaphoreType.DMA,
            pltpu.SemaphoreType.DMA,
            pltpu.SemaphoreType.DMA((2, OWN)),
            pltpu.SemaphoreType.DMA((2, OWN)),
        ],
        compiler_params=pltpu.CompilerParams(collective_id=0, has_side_effects=True, vmem_limit_bytes=62 * 1024 * 1024),
        name="duct",
    )(
        moments.reshape(MOMENTS * OWN, LINES),
        mask,
        coefficients,
        rates.reshape(1, MOMENTS),
        *constants,
    )
    return out.reshape(MOMENTS, OWN, LINES)


def solution(mesh):
    in_specs = (P(None, "wa", "gy"), P("wa", "gy"), P(), P())
    return jax.shard_map(local, mesh=mesh, in_specs=in_specs, out_specs=P(None, "wa", "gy"), check_vma=False)
```
